128 devices in a mesh: shard: 128 (over x, y, z, core).
Axes of the slice: x: 4, y: 4, z: 4, core: 2. Of those that a mesh axis runs over, the one named last changes fastest.
Arguments:
- embeddings: bfloat16 [262144, 1024], P('shard'), may hold values from -6 to 6
- block_rows: int32 [2048], P('shard'), may hold values from 1 to 128, 196608 in all
- pairs: int32 [65536, 3], P('shard'), may hold values from 0 to 2047, as said below
Outputs:
- best: float32 [2048, 128], P('shard')
The draws below stay inside these ranges and needn't reach their ends.
Inputs may be any that keep to these rules, and one draw needn't show every extreme that they name: `pairs`: entries d * 512 to (d + 1) * 512 - 1 are device d's. Each is (row block, column block, scorer); the scorer is d for a live entry and 128 for an unused one. The column block is always one of device d's blocks; the row block is one of device d's or of another device. Exactly 64 entries of device d have a row block of another device, all live, each from a different device; and the blocks of each device are row blocks of such entries of exactly 64 other devices. Live entries of one device number 64 to 512, and some device has 512.
All inputs are finite; a program needn't handle non-finite values. No bound on the sum of `block_rows` on one device may be relied on, other than what follows from the above.
Results may differ from the reference program's by a relative error of at most 0.0003.
Values may be sent and summed in bfloat16 or wider, within the bound.
No kernel may reach another device: no remote copies, remote signals or barrier semaphores. Data moves between devices by JAX's collectives and lax.ppermute only.
A program may use at most 256 MiB of HBM per device.

```python
import math
import jax
import jax.numpy as jnp
import numpy as np
from jax import lax

D = 1024
BR = 128
BPD = 16
PEERS = 64
PSLOT = 512
BLOCKS = 2048
N_SHARD = 128


def draw_pairs(key, part):
    key = jax.random.fold_in(key, 7)
    keys = jax.random.split(key, 8)
    device = jnp.arange(N_SHARD, dtype=jnp.int32)
    common = jax.random.permutation(keys[0], N_SHARD - 1)[:PEERS].astype(jnp.int32) + 1
    owner = (device[:, None] + common[None, :]) % N_SHARD
    far_rows = owner * BPD + jax.random.randint(keys[1], (N_SHARD, PEERS), 0, BPD)
    far_cols = device[:, None] * BPD + jax.random.randint(keys[2], (N_SHARD, PEERS), 0, BPD)
    extra = PSLOT - PEERS
    near_rows = device[:, None] * BPD + jax.random.randint(keys[3], (N_SHARD, extra), 0, BPD)
    near_cols = device[:, None] * BPD + jax.random.randint(keys[4], (N_SHARD, extra), 0, BPD)
    counts = jax.random.randint(keys[5], (N_SHARD,), 0, extra + 1)
    counts = counts.at[jax.random.randint(keys[6], (), 0, N_SHARD)].set(extra)
    live = jnp.arange(extra, dtype=jnp.int32)[None, :] < counts[:, None]
    near_scorer = jnp.where(live, device[:, None], N_SHARD)
    far_scorer = jnp.broadcast_to(device[:, None], (N_SHARD, PEERS))
    rows = jnp.concatenate([far_rows, near_rows], axis=1)
    cols = jnp.concatenate([far_cols, near_cols], axis=1)
    scorer = jnp.concatenate([far_scorer, near_scorer], axis=1)
    order = jax.vmap(lambda k: jax.random.permutation(k, PSLOT))(jax.random.split(keys[7], N_SHARD))
    rows = jnp.take_along_axis(rows, order, axis=1)
    cols = jnp.take_along_axis(cols, order, axis=1)
    scorer = jnp.take_along_axis(scorer, order, axis=1)
    return jnp.stack([rows, cols, scorer], axis=-1).reshape(N_SHARD * PSLOT, 3).astype(jnp.int32)


def steps_of(rng, extent, pieces, low, largest):
    loudness = 1.0
    for dim, shards_of in pieces:
        steps = jax.random.uniform(jax.random.fold_in(jax.random.fold_in(rng, 6), dim), (shards_of,), jnp.float32, low / len(pieces), largest / len(pieces))
        loudness = loudness * jnp.repeat(jnp.exp(steps), extent[dim] // shards_of).reshape((-1,) + (1,) * (len(extent) - 1 - dim))
    return loudness


def split_up(amount, total, limit, skew):
    portions = [(1 << 20) // math.isqrt(standing ** skew) + 1 for standing in range(2, amount + 1)]
    surplus, given = total - limit - (amount - 1), [1] * (amount - 1)
    while surplus > 0:
        free = [i for i in range(amount - 1) if given[i] < limit]
        whole, remaining = sum([portions[i] for i in free]), surplus
        for i in free:
            more = min(limit - given[i], max(1, remaining * portions[i] // whole), surplus)
            given[i] = given[i] + more
            surplus = surplus - more
    return np.array([limit] + given)


def uneven(stream_key, number_of, total, bound, slope):
    if number_of == 2:
        one = jax.random.randint(stream_key, (), max(1, total - bound), min(bound, total - 1) + 1)
        return jnp.stack([one, total - one])
    lengths = jnp.asarray(split_up(number_of, total, bound, slope), jnp.int32)
    pairs = (number_of - 1) // 2
    source_of, taker = lengths[1:1 + 2 * pairs:2], lengths[2:2 + 2 * pairs:2]
    margin = jnp.minimum(source_of - 1, bound - taker)
    shifted = jax.random.randint(jax.random.fold_in(stream_key, 1), (pairs,), 0, 1 << 20) % (margin + 1)
    lengths = lengths.at[1:1 + 2 * pairs:2].set(source_of - shifted).at[2:2 + 2 * pairs:2].set(taker + shifted)
    return lengths[jax.random.permutation(jax.random.fold_in(stream_key, 2), number_of)]


def gaussian(own_key, shape, spread, bound, cuts=(), held_as=jnp.bfloat16):
    result = spread * jax.random.normal(own_key, shape, jnp.float32)
    if cuts:
        result = result * steps_of(own_key, shape, cuts, -0.22, 0.18)
    return jnp.clip(result, -bound, bound).astype(held_as)


def setup_inputs(seed: int = 0) -> dict:
    arg_keys = jax.random.split(jax.random.key(seed), 4)
    return {
        "embeddings": gaussian(arg_keys[0], (BLOCKS * BR, D), 1.0, 6.0, ((0, 128),)),
        "block_rows": uneven(arg_keys[1], BLOCKS, BLOCKS * BR * 3 // 4, BR, 0).astype(jnp.int32),
        "pairs": draw_pairs(jax.random.fold_in(arg_keys[3], 71), 0),
    }


def reference(embeddings, block_rows, pairs):
    values = embeddings.astype(jnp.float32)
    scaled = values * lax.rsqrt(lax.optimization_barrier(jnp.sum(values * values, axis=-1, keepdims=True)) + 1e-06)
    unit = scaled.astype(jnp.bfloat16).reshape(BLOCKS, BR, D)
    groups = pairs.reshape(-1, 16, 3)
    index = jnp.arange(BR, dtype=jnp.int32)
    diagonal = index[:, None] == index[None, :]

    def step(best, group):
        row_block = group[:, 0].astype(jnp.int32)
        col_block = group[:, 1].astype(jnp.int32)
        alive = group[:, 2] < N_SHARD
        rows = unit[row_block].astype(jnp.float32)
        cols = unit[col_block].astype(jnp.float32)
        scores = jnp.einsum('gid,gjd->gij', rows, cols)
        row_count = block_rows[row_block]
        col_count = block_rows[col_block]
        keep = (index[None, :, None] < row_count[:, None, None]) & (index[None, None, :] < col_count[:, None, None])
        keep = keep & alive[:, None, None]
        keep = keep & ~((row_block == col_block)[:, None, None] & diagonal[None])
        masked = jnp.where(keep, scores, -1.0)
        best = best.at[row_block].max(masked.max(axis=2))
        best = best.at[col_block].max(masked.max(axis=1))
        return (best, None)
    start = jnp.full((BLOCKS, BR), -1.0, jnp.float32)
    best, _ = lax.scan(step, start, groups)
    return best
```

```python
import functools

import jax
import jax.numpy as jnp
from jax import lax
from jax.experimental import pallas as pl
from jax.experimental.pallas import tpu as pltpu
from jax.sharding import PartitionSpec as P

PARTS = 2


def normalize_kernel(values_ref, unit_ref):
    values = values_ref[...].astype(jnp.float32)
    total = jnp.sum(values * values, axis=-1, keepdims=True)
    unit_ref[...] = (values * lax.rsqrt(total + 1e-06)).astype(jnp.bfloat16)


def normalize(embeddings):
    rows, depth = embeddings.shape
    step = 256
    return pl.pallas_call(
        normalize_kernel,
        grid=(rows // step,),
        in_specs=[pl.BlockSpec((step, depth), lambda i: (i, 0))],
        out_specs=pl.BlockSpec((step, depth), lambda i: (i, 0)),
        out_shape=jax.ShapeDtypeStruct((rows, depth), jnp.bfloat16),
        name="normalize",
    )(embeddings)


def pack_kernel(group, chosen, unit_ref, out_ref):
    base = pl.program_id(0) * group
    for k in range(group):
        out_ref[k] = unit_ref[chosen[base + k]]


def pack(chosen, unit, part):
    blocks, width, depth = unit.shape
    slots = chosen.shape[0]
    rows = width // PARTS
    group = 8
    return pl.pallas_call(
        functools.partial(pack_kernel, group),
        grid_spec=pltpu.PrefetchScalarGridSpec(
            num_scalar_prefetch=1,
            grid=(slots // group,),
            in_specs=[pl.BlockSpec((blocks, rows, depth), lambda i, c: (0, part, 0))],
            out_specs=pl.BlockSpec((group, rows, depth), lambda i, c: (i, 0, 0)),
        ),
        out_shape=jax.ShapeDtypeStruct((slots, rows, depth), jnp.bfloat16),
        compiler_params=pltpu.CompilerParams(vmem_limit_bytes=40 * 1024 * 1024),
        name="pack",
    )(chosen, unit)


def score_kernel(group, first, mine, mine_rows, theirs_rows, unit_ref, arrived_ref, back_ref, best_ref, held):
    step = pl.program_id(0)
    blocks, width, _ = unit_ref.shape
    rows = arrived_ref.shape[1]

    @pl.when(step == 0)
    def _():
        held[...] = jnp.full(held.shape, -1.0, jnp.float32)

    i = lax.broadcasted_iota(jnp.int32, (width, rows), 0)
    j = lax.broadcasted_iota(jnp.int32, (width, rows), 1) + first
    back_ref[...] = jnp.full(back_ref.shape, -1.0, jnp.float32)
    for k in range(group):
        slot = step * group + k

        @pl.when(theirs_rows[slot] > first)
        def _():
            block = mine[slot]
            scores = lax.dot_general(
                unit_ref[block], arrived_ref[k], (((1,), (1,)), ((), ())), preferred_element_type=jnp.float32
            )
            keep = (i < mine_rows[slot]) & (j < theirs_rows[slot])
            scores = jnp.where(keep, scores, -1.0)
            back_ref[pl.ds(k, 1), :] = jnp.max(scores, axis=0, keepdims=True)
            held[block] = jnp.maximum(held[block], scores)

    @pl.when(step == pl.num_programs(0) - 1)
    def _():
        for b in range(blocks):
            best_ref[pl.ds(b, 1), :] = jnp.max(held[b].T, axis=0, keepdims=True)


def score(first, mine, mine_rows, theirs_rows, unit, arrived):
    blocks, width, depth = unit.shape
    slots, rows, _ = arrived.shape
    group = 8
    return pl.pallas_call(
        functools.partial(score_kernel, group, first),
        grid_spec=pltpu.PrefetchScalarGridSpec(
            num_scalar_prefetch=3,
            grid=(slots // group,),
            in_specs=[
                pl.BlockSpec((blocks, width, depth), lambda i, *_: (0, 0, 0)),
                pl.BlockSpec((group, rows, depth), lambda i, *_: (i, 0, 0)),
            ],
            out_specs=[
                pl.BlockSpec((group, rows), lambda i, *_: (i, 0)),
                pl.BlockSpec((blocks, width), lambda i, *_: (0, 0)),
            ],
            scratch_shapes=[pltpu.VMEM((blocks, width, rows), jnp.float32)],
        ),
        out_shape=[
            jax.ShapeDtypeStruct((slots, rows), jnp.float32),
            jax.ShapeDtypeStruct((blocks, width), jnp.float32),
        ],
        compiler_params=pltpu.CompilerParams(vmem_limit_bytes=40 * 1024 * 1024),
        name="score",
    )(mine, mine_rows, theirs_rows, unit, arrived)


def one_hot(index, count, valid):
    return (index[:, None] == jnp.arange(count, dtype=jnp.int32)[None, :]) & valid[:, None]


def pick(index, values):
    hit = index[:, None] == jnp.arange(values.shape[-1], dtype=jnp.int32)[None, :]
    return jnp.sum(jnp.where(hit, values, 0), axis=1)


def fold_maxima(selector, maxima):
    spread = jnp.where(selector[:, :, None], maxima[:, None, :], -1.0)
    return spread.max(axis=0)


def local_maxima(unit, block_rows, linked):
    blocks, width, depth = unit.shape
    total = blocks * width
    flat = unit.reshape(total, depth)
    live_flat = (jnp.arange(width, dtype=jnp.int32)[None, :] < block_rows[:, None]).reshape(total)
    linked_rows = jnp.repeat(linked, width, axis=0)
    span = min(512, total)
    columns = jnp.arange(total, dtype=jnp.int32)

    def tile(number):
        start = number * span
        query = lax.dynamic_slice_in_dim(flat, start, span, 0)
        scores = lax.dot_general(query, flat, (((1,), (1,)), ((), ())), preferred_element_type=jnp.float32)
        ids = start + jnp.arange(span, dtype=jnp.int32)
        link = jnp.repeat(lax.dynamic_slice_in_dim(linked_rows, start, span, 0), width, axis=1)
        keep = link & live_flat[None, :] & lax.dynamic_slice_in_dim(live_flat, start, span, 0)[:, None]
        keep = keep & (ids[:, None] != columns[None, :])
        return jnp.where(keep, scores, -1.0).max(axis=1)

    result = lax.map(tile, jnp.arange(total // span, dtype=jnp.int32))
    return result.reshape(blocks, width)


def on_device(embeddings, block_rows, pairs):
    blocks = block_rows.shape[0]
    width = embeddings.shape[0] // blocks
    peers = lax.axis_size("shard")
    myself = lax.axis_index("shard")
    row_block, col_block = pairs[:, 0], pairs[:, 1]
    alive = pairs[:, 2] == myself
    owner = row_block // blocks
    remote = alive & (owner != myself)
    row_local, col_local = row_block % blocks, col_block % blocks
    code = row_local * blocks + col_local
    wanted = jnp.max(jnp.where(one_hot(owner, peers, remote), code[:, None], -1), axis=0)
    told = lax.all_gather(jnp.concatenate([wanted, block_rows])[None], "shard", axis=0, tiled=True)

    unit = normalize(embeddings).reshape(blocks, width, -1)
    chosen = jnp.maximum(wanted, 0) % blocks
    arrived = []
    for part in range(PARTS):
        outgoing = pack(chosen, unit, part)
        arrived.append(lax.all_to_all(outgoing, "shard", split_axis=0, concat_axis=0, tiled=True))

    asked = lax.dynamic_slice_in_dim(told, myself, 1, 1)[:, 0]
    valid = asked >= 0
    mine = jnp.maximum(asked, 0) // blocks
    theirs_rows = jnp.where(valid, pick(jnp.maximum(asked, 0) % blocks, told[:, peers:]), 0)
    mine_rows = pick(mine, block_rows[None, :])

    nearby = alive & ~remote
    row_table = one_hot(row_local, blocks, nearby).astype(jnp.float32)
    col_table = one_hot(col_local, blocks, nearby).astype(jnp.float32)
    adjacency = (
        lax.dot_general(row_table, col_table, (((0,), (0,)), ((), ())), preferred_element_type=jnp.float32) > 0.5
    )
    best = local_maxima(unit, block_rows, adjacency | adjacency.T)

    back = []
    for part in range(PARTS):
        part_back, part_best = score(
            part * (width // PARTS), mine, mine_rows, theirs_rows, unit, arrived[part]
        )
        back.append(part_back)
        best = jnp.maximum(best, part_best)
    returned = lax.all_to_all(
        jnp.concatenate(back, axis=1), "shard", split_axis=0, concat_axis=0, tiled=True
    )
    return jnp.maximum(best, fold_maxima(one_hot(chosen, blocks, wanted >= 0), returned))


def solution(mesh):
    placed = (P("shard", None), P("shard"), P("shard", None))
    return jax.shard_map(
        on_device, mesh=mesh, in_specs=placed, out_specs=P("shard", None), check_vma=False
    )
```

```python
import functools

import jax
import jax.numpy as jnp
import numpy as np
from jax import lax
from jax.experimental import pallas as pl
from jax.experimental.pallas import tpu as pltpu
from jax.sharding import PartitionSpec as P

UNIT = 16
ITEM = 4
SHARE = 8
MIB = 1024 * 1024


def normalize_kernel(values_ref, unit_ref):
    values = values_ref[...].astype(jnp.float32)
    total = jnp.sum(values * values, axis=-1, keepdims=True)
    unit_ref[...] = (values * lax.rsqrt(total + 1e-06)).astype(jnp.bfloat16)


def normalize(embeddings):
    rows, depth = embeddings.shape
    step = 256
    return pl.pallas_call(
        normalize_kernel,
        grid=(rows // step,),
        in_specs=[pl.BlockSpec((step, depth), lambda i: (i, 0))],
        out_specs=pl.BlockSpec((step, depth), lambda i: (i, 0)),
        out_shape=jax.ShapeDtypeStruct((rows, depth), jnp.bfloat16),
        name="normalize",
    )(embeddings)


def nearby_kernel(first, second, linked, counts, unit_ref, best_ref, held):
    step = pl.program_id(0)
    blocks = best_ref.shape[0]
    width = 128

    @pl.when(step == 0)
    def _():
        held[...] = jnp.full(held.shape, -1.0, jnp.float32)
        best_ref[...] = jnp.full(best_ref.shape, -1.0, jnp.float32)

    left, right = first[step], second[step]
    i = lax.broadcasted_iota(jnp.int32, (width, width), 0)
    j = lax.broadcasted_iota(jnp.int32, (width, width), 1)
    rows = unit_ref[pl.ds(pl.multiple_of(left * 256, 256), 256), :]
    cols = unit_ref[pl.ds(pl.multiple_of(right * 256, 256), 256), :]
    scores = lax.dot_general(rows, cols, (((1,), (1,)), ((), ())), preferred_element_type=jnp.float32)
    for a in range(2):
        for b in range(2):
            r, c = left * 2 + a, right * 2 + b
            limit = jnp.where(linked[r * blocks + c] > 0, counts[r], 0)
            keep = (i < limit) & (j < counts[c]) & ((r != c) | (i != j))
            part = jnp.where(keep, scores[a * width : (a + 1) * width, b * width : (b + 1) * width], -1.0)
            held[r] = jnp.maximum(held[r], part)
            best_ref[pl.ds(c, 1), :] = jnp.maximum(best_ref[pl.ds(c, 1), :], jnp.max(part, axis=0, keepdims=True))

    @pl.when(step == pl.num_programs(0) - 1)
    def _():
        for b in range(blocks):
            best_ref[pl.ds(b, 1), :] = jnp.maximum(
                best_ref[pl.ds(b, 1), :], jnp.max(held[b].T, axis=0, keepdims=True)
            )


def nearby_maxima(unit, counts, linked):
    rows, depth = unit.shape
    blocks = counts.shape[0]
    sides = rows // 256
    first, second = np.triu_indices(sides)
    return pl.pallas_call(
        nearby_kernel,
        grid_spec=pltpu.PrefetchScalarGridSpec(
            num_scalar_prefetch=4,
            grid=(len(first),),
            in_specs=[pl.BlockSpec((rows, depth), lambda i, *_: (0, 0))],
            out_specs=pl.BlockSpec((blocks, rows // blocks), lambda i, *_: (0, 0)),
            scratch_shapes=[pltpu.VMEM((blocks, 128, 128), jnp.float32)],
        ),
        out_shape=jax.ShapeDtypeStruct((blocks, rows // blocks), jnp.float32),
        compiler_params=pltpu.CompilerParams(vmem_limit_bytes=32 * MIB),
        name="nearby",
    )(
        jnp.asarray(first, jnp.int32),
        jnp.asarray(second, jnp.int32),
        linked.astype(jnp.int32).reshape(-1),
        counts,
        unit,
    )


def exact_dot(a, b):
    return jnp.dot(
        a.astype(jnp.float32).astype(jnp.bfloat16),
        b.astype(jnp.float32).astype(jnp.bfloat16),
        preferred_element_type=jnp.float32,
    ).astype(jnp.int32)


def flip(a):
    return a.astype(jnp.float32).T.astype(jnp.int32)


def plan_kernel(
    direct, items, chips, me_ref, pair_ref, count_ref, count_t_ref,
    send_ref, far_ref, seg_ref, far_seg_ref, hand_ref, target_ref, back_ref, fits_ref,
    w_lo, w_hi, sums, mine,
):
    device = me_ref[0]
    chip, core = device // 2, device % 2
    devices = 2 * chips
    flat = (chips, chips)
    pair = pair_ref[...]
    code = jnp.maximum(pair, 0)
    row_of, col_of = code >> 4, code & 15
    row_count = jnp.zeros(pair.shape, jnp.int32)
    col_count = jnp.zeros(pair.shape, jnp.int32)
    for l in range(16):
        row_count = jnp.where(row_of == l, count_t_ref[pl.ds(l, 1), :], row_count)
        col_count = jnp.where(col_of == l, count_ref[:, l : l + 1], col_count)

    xs = lax.broadcasted_iota(jnp.int32, (chips, devices), 0)
    ds = lax.broadcasted_iota(jnp.int32, (chips, devices), 1)
    pick = [(ds == 2 * xs + i).astype(jnp.int32) for i in range(2)]
    pick_t = [flip(p) for p in pick]

    def split(values):
        half = [exact_dot(p, values) for p in pick]
        return [[exact_dot(half[i], pick_t[j]) for j in range(2)] for i in range(2)]

    asked = {"code": split(pair + 1), "row": split(row_count), "col": split(col_count)}
    asked_t = {k: [[flip(v[j][i]) for j in range(2)] for i in range(2)] for k, v in asked.items()}

    x = lax.broadcasted_iota(jnp.int32, flat, 0)
    y = lax.broadcasted_iota(jnp.int32, flat, 1)
    low, same = x <= y, x == y
    edges = []
    for kind in range(2):
        for p in range(2):
            for q in range(2):
                first, second = (asked_t, asked) if kind == 0 else (asked, asked_t)
                here = {k: jnp.where(low, first[k][p][q], second[k][q][p]) for k in asked}
                exists = here["code"] > 0
                if kind == 1:
                    exists = exists & ~same
                number = jnp.maximum(here["code"] - 1, 0)
                r, c = number >> 4, number & 15
                side = jnp.where(low, p, q) * 16
                other = jnp.where(low, q, p) * 16
                owns_row = low if kind == 0 else ~low
                own_block = side + jnp.where(owns_row, r, c)
                other_block = other + jnp.where(owns_row, c, r)
                own_rows = jnp.where(exists, jnp.where(owns_row, here["row"], here["col"]), 0)
                other_rows = jnp.where(exists, jnp.where(owns_row, here["col"], here["row"]), 0)
                edges.append((exists, own_block, other_block, own_rows, other_rows))
    for e, (exists, _, _, own_rows, other_rows) in enumerate(edges):
        own_units, other_units = (own_rows + 15) >> 4, (other_rows + 15) >> 4
        w_lo[e] = jnp.where(low, own_units, other_units)
        w_hi[e] = jnp.where(low, other_units, own_units)

    for half in range(2):
        for choice in range(16):
            up = jnp.zeros(flat, jnp.int32)
            down = jnp.zeros(flat, jnp.int32)
            for b in range(4):
                if choice >> b & 1:
                    up = up + w_lo[half * 4 + b]
                else:
                    down = down + w_hi[half * 4 + b]
            sums[half, choice] = up
            sums[2 + half, choice] = down

    def try_half(a, least):
        up_a, down_a = sums[0, a], sums[2, a]
        for b in range(16):
            up, down = up_a + sums[1, b], down_a + sums[3, b]
            over_up, over_down = jnp.maximum(up - 2 * direct, 0), jnp.maximum(down - 2 * direct, 0)
            far = ((over_up + 3) >> 2) + ((over_down + 3) >> 2)
            rank = (((far * 64 + over_up + over_down) * 128) + jnp.maximum(up, down)) * 256 + (b * 16 + a)
            least = jnp.minimum(least, rank)
        return least

    least = lax.fori_loop(0, 16, try_half, jnp.full(flat, 2**30, jnp.int32))
    chosen = jnp.where(same, 255, least & 255)

    out_total = jnp.zeros(flat, jnp.int32)
    in_total = jnp.zeros(flat, jnp.int32)
    for e, (exists, own_block, other_block, own_rows, other_rows) in enumerate(edges):
        bit = (chosen >> e) & 1
        sends = exists & ((bit == 1) == low)
        out_units = jnp.where(sends, (own_rows + 15) >> 4, 0)
        in_rows = jnp.where(same, own_rows, other_rows)
        in_units = jnp.where((exists & ~sends) | same, (in_rows + 15) >> 4, 0)
        out_total = out_total + out_units
        in_total = in_total + in_units
        mine[e] = out_units
        mine[8 + e] = own_block ^ (core * 16)
        mine[16 + e] = in_units
        mine[24 + e] = jnp.where(same, other_block, own_block) ^ (core * 16)
        mine[32 + e] = in_rows
    mine[40] = out_total
    mine[41] = in_total

    over = jnp.maximum(out_total - 2 * direct, 0)
    far = (over + 3) >> 2
    before = exact_dot(far, (x < y).astype(jnp.int32))
    total = jnp.sum(far, axis=1, keepdims=True)
    at_self = jnp.sum(jnp.where(same, before, 0), axis=1, keepdims=True)
    rank = before - at_self + jnp.where(y < x, total, 0)
    number, place = [], []
    worst = jnp.max((total + 1) >> 1)
    for k in range(2):
        number.append((far + ((rank & 1) == k).astype(jnp.int32)) >> 1)
        place.append(exact_dot((y < x).astype(jnp.int32), number[k]))
        worst = jnp.maximum(worst, jnp.max(jnp.sum(number[k], axis=0, keepdims=True)))
    fits_ref[0] = (worst <= items).astype(jnp.int32)
    odd = core == 1
    number = jnp.where(odd, number[1], number[0])
    place = jnp.where(odd, place[1], place[0])
    skip = ((rank & 1) != core).astype(jnp.int32)
    number_t, place_t, rank_t, skip_t, far_t = flip(number), flip(place), flip(rank), flip(skip), flip(far)
    for k, v in enumerate((number, rank, skip, far, number_t, place_t, rank_t, skip_t, far_t)):
        mine[42 + k] = v
    own = pl.ds(chip, 1)

    out_units = [mine[e, own, :] for e in range(SHARE)]
    out_block = [mine[8 + e, own, :] for e in range(SHARE)]
    in_units = [mine[16 + e, own, :] for e in range(SHARE)]
    in_block = [mine[24 + e, own, :] for e in range(SHARE)]
    in_rows = [mine[32 + e, own, :] for e in range(SHARE)]
    out_total, in_total = mine[40, own, :], mine[41, own, :]
    number, rank, skip, far, number_t, place_t, rank_t, skip_t, far_t = (mine[42 + k, own, :] for k in range(9))

    def lane(total):
        plain = jnp.minimum(total, 2 * direct)
        half = (plain + 1) >> 1
        return jnp.where(odd, half, 0), jnp.where(odd, plain - half, half)

    def unit_at(position, valid):
        value = jnp.full(position.shape, -1, jnp.int32)
        start = jnp.zeros((1, chips), jnp.int32)
        for e in range(SHARE):
            hit = valid & (position >= start) & (position < start + out_units[e])
            value = jnp.where(hit, out_block[e] * 8 + position - start, value)
            start = start + out_units[e]
        return value

    begin, length = lane(out_total)
    step = lax.broadcasted_iota(jnp.int32, (direct, chips), 0)
    plain = unit_at(begin + step, step < length)
    send_ref[...] = jnp.maximum(plain, 0)
    target_ref[pl.ds(0, direct), :] = plain

    begin, length = lane(in_total)
    start = jnp.zeros((1, chips), jnp.int32)
    starts = []
    for e in range(SHARE):
        starts.append(start)
        top = jnp.maximum(start, begin) - begin
        end = jnp.minimum(start + in_units[e], begin + length) - begin
        last = jnp.minimum(UNIT * end, UNIT * (start - begin) + in_rows[e])
        seg_ref[pl.ds(e, 1), :] = jnp.where(end > top, (in_block[e] << 16) + (top << 10) + last, 0)
        start = start + in_units[e]

    if items:
        slot = lax.broadcasted_iota(jnp.int32, (items, chips), 0)
        sixteen = lax.broadcasted_iota(jnp.int32, (16, chips), 0) + 2 * direct
        beyond = unit_at(sixteen, sixteen < out_total)
        for p in range(ITEM):
            value = jnp.zeros((items, 1), jnp.int32)
            for t in range(4):
                hit = (rank + t == 2 * slot + core) & (t < far)
                row = jnp.maximum(beyond[4 * t + p : 4 * t + p + 1], 0)
                value = value + jnp.sum(jnp.where(hit, row, 0), axis=1, keepdims=True)
            far_ref[:, p : p + 1] = value
        for k in range(2):
            for p in range(ITEM):
                even, uneven = beyond[8 * k + p : 8 * k + p + 1], beyond[8 * k + 4 + p : 8 * k + 5 + p]
                target_ref[pl.ds(direct + 4 * k + p, 1), :] = jnp.where(
                    k < number, jnp.where(skip == 0, even, uneven), -1
                )
            back_ref[pl.ds(k, 1), :] = jnp.where(k < number_t, place_t + k, -1)
        hits = [
            (place_t + (t >> 1) == slot) & ((t & 1) == skip_t) & (t < far_t) for t in range(4)
        ]
        for e in range(SHARE):
            value = jnp.zeros((items, 1), jnp.int32)
            for t in range(4):
                offset = starts[e] - (2 * direct + 4 * t)
                top = jnp.clip(offset, 0, 4)
                end = jnp.clip(offset + in_units[e], 0, 4)
                last = jnp.minimum(UNIT * end, UNIT * offset + in_rows[e])
                made = jnp.where(end > top, (in_block[e] << 16) + (top << 10) + last, 0)
                value = value + jnp.sum(jnp.where(hits[t], made, 0), axis=1, keepdims=True)
            far_seg_ref[:, e : e + 1] = value
        number_t, place_t, rank_t, skip_t = (mine[42 + k] for k in (4, 5, 6, 7))
        for q in range(items):
            value = jnp.zeros(flat, jnp.int32)
            for k in range(2):
                hit = (place_t + k == q) & (k < number_t)
                value = value + jnp.where(hit, y * items + ((rank_t + skip_t + 2 * k) >> 1), 0)
            hand_ref[:, q : q + 1] = jnp.sum(value, axis=1, keepdims=True)


def make_plan(direct, items, told, device):
    devices, columns = told.shape
    chips = devices // 2
    blocks = columns - devices
    ints = lambda *shape: jax.ShapeDtypeStruct(shape, jnp.int32)
    vmem = pl.BlockSpec(memory_space=pltpu.VMEM)
    some = max(items, 8)
    return pl.pallas_call(
        functools.partial(plan_kernel, direct, items, chips),
        in_specs=[pl.BlockSpec(memory_space=pltpu.SMEM), vmem, vmem, vmem],
        out_specs=[vmem] * 7 + [pl.BlockSpec(memory_space=pltpu.SMEM)],
        out_shape=[
            ints(direct, chips),
            ints(some, ITEM),
            ints(SHARE, chips),
            ints(some, SHARE),
            ints(chips, some),
            ints(direct + 8, chips),
            ints(2, chips),
            ints(1),
        ],
        scratch_shapes=[
            pltpu.VMEM((SHARE, chips, chips), jnp.int32),
            pltpu.VMEM((SHARE, chips, chips), jnp.int32),
            pltpu.VMEM((4, 16, chips, chips), jnp.int32),
            pltpu.VMEM((51, chips, chips), jnp.int32),
        ],
        compiler_params=pltpu.CompilerParams(vmem_limit_bytes=32 * MIB),
        name="plan",
    )(device.reshape(1), told[:, :devices], told[:, devices:], told[:, devices:].T)


def fetch(near_ref, far_ref, held, sems):
    half = near_ref.shape[0]
    copies = [
        pltpu.make_async_copy(near_ref, held.at[pl.ds(0, half)], sems.at[0]),
        pltpu.make_async_copy(far_ref, held.at[pl.ds(half, half)], sems.at[1]),
    ]
    for copy in copies:
        copy.start()
    for copy in copies:
        copy.wait()


def pack_kernel(group, direct, items, send, far, near_ref, far_ref, out_ref, held, gathered, turned, sems):
    step = pl.program_id(0)
    chips = pl.num_programs(0) * group

    @pl.when(step == 0)
    def _():
        fetch(near_ref, far_ref, held, sems)
        if items:
            for q in range(items):
                for p in range(ITEM):
                    gathered[pl.ds(q * ITEM * UNIT + p * UNIT, UNIT), :] = held[far[q * ITEM + p]]
            rows = items * chips
            o = lax.broadcasted_iota(jnp.int32, (128, rows), 0)
            i = lax.broadcasted_iota(jnp.int32, (128, rows), 1)
            for part in range(rows // 128):
                at = o + part * 128
                take = ((at % items) * chips + at // items == i).astype(jnp.float32).astype(jnp.bfloat16)
                turned[pl.ds(part * 128, 128), :] = jnp.dot(
                    take, gathered[...], preferred_element_type=jnp.float32
                ).astype(jnp.bfloat16)

    for k in range(group):
        slot = step * group + k
        for p in range(direct):
            out_ref[k, pl.ds(p * UNIT, UNIT), :] = held[send[p * chips + slot]]
        if items:
            out_ref[k, pl.ds(direct * UNIT, items), :] = turned[pl.ds(pl.multiple_of(slot * items, items), items), :]


def pack(direct, items, send, far, near_units, far_units):
    units, _, depth = near_units.shape
    chips = send.shape[1]
    rows = direct * UNIT + items
    group = 4
    some = max(items, 16)
    return pl.pallas_call(
        functools.partial(pack_kernel, group, direct, items),
        grid_spec=pltpu.PrefetchScalarGridSpec(
            num_scalar_prefetch=2,
            grid=(chips // group,),
            in_specs=[pl.BlockSpec(memory_space=pl.ANY)] * 2,
            out_specs=pl.BlockSpec((group, rows, depth), lambda i, *_: (i, 0, 0)),
            scratch_shapes=[
                pltpu.VMEM((2 * units, UNIT, depth), jnp.bfloat16),
                pltpu.VMEM((some * ITEM * UNIT, depth), jnp.bfloat16),
                pltpu.VMEM((some * chips, depth), jnp.bfloat16),
                pltpu.SemaphoreType.DMA((2,)),
            ],
        ),
        out_shape=jax.ShapeDtypeStruct((chips, rows, depth), jnp.bfloat16),
        compiler_params=pltpu.CompilerParams(vmem_limit_bytes=40 * MIB),
        name="pack",
    )(send.reshape(-1), far.reshape(-1), near_units, far_units)


def score_kernel(group, by_edge, seg, counts, near_ref, far_ref, arrived_ref, back_ref, best_ref, held, row_best, sems):
    step = pl.program_id(0)
    rows = arrived_ref.shape[1]
    width = held.shape[1]
    slots = pl.num_programs(0) * group

    @pl.when(step == 0)
    def _():
        fetch(near_ref, far_ref, held, sems)
        best_ref[...] = jnp.full(best_ref.shape, -1.0, jnp.float32)

    i = lax.broadcasted_iota(jnp.int32, (rows, width), 0)
    j = lax.broadcasted_iota(jnp.int32, (rows, width), 1)
    for k in range(group):
        slot = step * group + k
        row_best[k] = jnp.full((rows, width), -1.0, jnp.float32)

        def segment(e, carry):
            made = seg[e * slots + slot] if by_edge else seg[slot * SHARE + e]

            @pl.when(made > 0)
            def _():
                block = made >> 16
                top = ((made >> 10) & 63) * UNIT
                scores = lax.dot_general(
                    arrived_ref[k], held[block], (((1,), (1,)), ((), ())), preferred_element_type=jnp.float32
                )
                keep = (i >= top) & (i < (made & 1023)) & (j < counts[block])
                scores = jnp.where(keep, scores, -1.0)
                row_best[k] = jnp.maximum(row_best[k], scores)
                best_ref[pl.ds(block, 1), :] = jnp.maximum(
                    best_ref[pl.ds(block, 1), :], jnp.max(scores, axis=0, keepdims=True)
                )

            return carry

        lax.fori_loop(0, SHARE, segment, 0)
        back_ref[pl.ds(k, 1), :] = jnp.max(row_best[k].T, axis=0, keepdims=True)


def score(seg, by_edge, counts, near, far, arrived, rows):
    blocks, width, depth = near.shape
    slots = arrived.shape[0]
    group = 8
    return pl.pallas_call(
        functools.partial(score_kernel, group, by_edge),
        grid_spec=pltpu.PrefetchScalarGridSpec(
            num_scalar_prefetch=2,
            grid=(slots // group,),
            in_specs=[pl.BlockSpec(memory_space=pl.ANY)] * 2
            + [pl.BlockSpec((group, rows, depth), lambda i, *_: (i, 0, 0))],
            out_specs=[
                pl.BlockSpec((group, rows), lambda i, *_: (i, 0)),
                pl.BlockSpec((2 * blocks, width), lambda i, *_: (0, 0)),
            ],
            scratch_shapes=[
                pltpu.VMEM((2 * blocks, width, depth), jnp.bfloat16),
                pltpu.VMEM((group, rows, width), jnp.float32),
                pltpu.SemaphoreType.DMA((2,)),
            ],
        ),
        out_shape=[
            jax.ShapeDtypeStruct((slots, rows), jnp.float32),
            jax.ShapeDtypeStruct((2 * blocks, width), jnp.float32),
        ],
        compiler_params=pltpu.CompilerParams(vmem_limit_bytes=48 * MIB),
        name="score",
    )(seg.reshape(-1), counts, near, far, arrived)


def one_hot(index, count, valid):
    return (index[:, None] == jnp.arange(count, dtype=jnp.int32)[None, :]) & valid[:, None]


def exchange(values, chips):
    groups = [[2 * x + c for x in range(chips)] for c in range(2)]
    return lax.all_to_all(values, "shard", split_axis=0, concat_axis=0, axis_index_groups=groups, tiled=True)


def far_maxima(direct, items, plan, counts, near, far):
    send, own_items, seg, far_seg, hand, target, item_back, _ = plan
    blocks, width, depth = near.shape
    chips = send.shape[1]
    outgoing = pack(
        direct, items, send, own_items,
        near.reshape(-1, UNIT, depth), far.reshape(-1, UNIT, depth),
    )
    arrived = exchange(outgoing, chips)
    rows = direct * UNIT
    if items:
        held = arrived[:, rows:, :].reshape(chips * items, depth)
        take = one_hot(hand.reshape(-1), chips * items, jnp.full((chips * items,), True))
        passed = jnp.dot(take.astype(jnp.bfloat16), held, preferred_element_type=jnp.bfloat16)
        relayed = exchange(passed.reshape(chips, items, depth), chips)
    back, best = score(seg, True, counts, near, far, arrived, rows)
    places = direct
    if items:
        relayed = relayed.swapaxes(0, 1)
        far_back, far_best = score(far_seg, False, counts, near, far, relayed, chips)
        best = jnp.maximum(best, far_best)
        hit = item_back.T[:, :, None] == jnp.arange(items, dtype=jnp.int32)[None, None, :]
        far_back = jnp.where(hit[..., None], far_back[None, None], -1.0).max(axis=2)
        back = jnp.concatenate([back, far_back.reshape(chips, -1)], axis=1)
        places = direct + 8
    returned = exchange(back, chips).reshape(chips, places, UNIT)
    spots = target[:places].T.reshape(-1)
    values = returned.reshape(-1, UNIT).T
    number = 2 * blocks * width // UNIT
    hit = spots[:, None] == jnp.arange(number, dtype=jnp.int32)[None, :]
    folded = jnp.where(hit[None], values[:, :, None], -1.0).max(axis=1)
    return jnp.maximum(best, folded.T.reshape(2 * blocks, width))


def on_device(embeddings, block_rows, pairs):
    blocks = block_rows.shape[0]
    width = embeddings.shape[0] // blocks
    peers = lax.axis_size("shard")
    myself = lax.axis_index("shard")
    swap = [(d, d ^ 1) for d in range(peers)]
    row_block, col_block = pairs[:, 0], pairs[:, 1]
    alive = pairs[:, 2] == myself
    owner = row_block // blocks
    remote = alive & (owner != myself)
    row_local, col_local = row_block % blocks, col_block % blocks
    code = row_local * blocks + col_local
    wanted = jnp.max(jnp.where(one_hot(owner, peers, remote), code[:, None], -1), axis=0)
    tell = jnp.concatenate([wanted, block_rows])[None]
    told = lax.all_to_all(
        jnp.broadcast_to(tell, (peers, tell.shape[1])), "shard", split_axis=0, concat_axis=0, tiled=True
    )

    unit = normalize(embeddings)
    near = unit.reshape(blocks, width, -1)
    far = lax.ppermute(near, "shard", swap)

    nearby = alive & ~remote
    row_table = one_hot(row_local, blocks, nearby).astype(jnp.float32)
    col_table = one_hot(col_local, blocks, nearby).astype(jnp.float32)
    adjacency = (
        lax.dot_general(row_table, col_table, (((0,), (0,)), ((), ())), preferred_element_type=jnp.float32) > 0.5
    )
    best = nearby_maxima(unit, block_rows, adjacency | adjacency.T)

    direct, items = 8, 16
    plan = make_plan(direct, items, told, myself)
    counts = jnp.concatenate([block_rows, lax.dynamic_slice_in_dim(told, myself ^ 1, 1, 0)[0, peers:]])
    near, far, best, plan, counts = lax.optimization_barrier((near, far, best, plan, counts))

    def usual():
        return far_maxima(direct, items, plan, counts, near, far)

    def roomy():
        return far_maxima(16, 0, make_plan(16, 0, told, myself), counts, near, far)

    both = lax.cond(plan[-1][0] > 0, usual, roomy)
    other = lax.ppermute(both[blocks:], "shard", swap)
    return jnp.maximum(best, jnp.maximum(both[:blocks], other))


def solution(mesh):
    placed = (P("shard", None), P("shard"), P("shard", None))
    return jax.shard_map(
        on_device, mesh=mesh, in_specs=placed, out_specs=P("shard", None), check_vma=False
    )
```

```python
import functools

import jax
import jax.numpy as jnp
import numpy as np
from jax import lax
from jax.experimental import pallas as pl
from jax.experimental.pallas import tpu as pltpu
from jax.sharding import PartitionSpec as P

UNIT = 16
CLASSES = 4
COLORS = 2 * CLASSES
LOG_COLORS = 3
PLANS = ((7, 16, 24), (8, 16, 16), (16, 0, 0))
SHARE = 8
MIB = 1024 * 1024


def turns(direct):
    return -(-(2 * 16 - 2 * direct) // COLORS)


def ask_kernel(me_ref, pairs_ref, rows_ref, tell_ref):
    device = me_ref[0]
    peers, _, columns = tell_ref.shape
    blocks = rows_ref.shape[1]
    row, col = pairs_ref[:, 0:1], pairs_ref[:, 1:2]
    owner = row >> 4
    far = (pairs_ref[:, 2:3] == device) & (owner != device)
    lane = lax.broadcasted_iota(jnp.int32, (row.shape[0], peers), 1)
    code = (row & 15) * 16 + (col & 15)
    wanted = jnp.max(jnp.where((owner == lane) & far, code, -1), axis=0, keepdims=True)
    tell = jnp.concatenate([wanted, rows_ref[...]], axis=1)
    tell_ref[...] = jnp.broadcast_to(tell[None], tell_ref.shape)


def ask(device, pairs, block_rows, peers):
    blocks = block_rows.shape[0]
    assert blocks == 16
    vmem = pl.BlockSpec(memory_space=pltpu.VMEM)
    return pl.pallas_call(
        ask_kernel,
        in_specs=[pl.BlockSpec(memory_space=pltpu.SMEM), vmem, vmem],
        out_specs=vmem,
        out_shape=jax.ShapeDtypeStruct((peers, 1, peers + blocks), jnp.int32),
        name="ask",
    )(device.reshape(1), pairs, block_rows.reshape(1, blocks))


def normalize_kernel(after_ref, values_ref, unit_ref):
    values = values_ref[...].astype(jnp.float32)
    total = jnp.sum(values * values, axis=-1, keepdims=True)
    unit_ref[...] = (values * lax.rsqrt(total + 1e-06)).astype(jnp.bfloat16)


def normalize(embeddings, after):
    rows, depth = embeddings.shape
    step = 512
    return pl.pallas_call(
        normalize_kernel,
        grid=(rows // step,),
        in_specs=[pl.BlockSpec(memory_space=pl.ANY), pl.BlockSpec((step, depth), lambda i: (i, 0))],
        out_specs=pl.BlockSpec((step, depth), lambda i: (i, 0)),
        out_shape=jax.ShapeDtypeStruct((rows, depth), jnp.bfloat16),
        cost_estimate=pl.CostEstimate(flops=4 * rows * depth, bytes_accessed=4 * rows * depth, transcendentals=rows),
        name="normalize",
    )(after, embeddings)


def nearby_kernel(first, second, linked, counts, unit_ref, best_ref, held):
    step = pl.program_id(0)
    blocks = best_ref.shape[0]
    width = 128

    @pl.when(step == 0)
    def _():
        held[...] = jnp.full(held.shape, -1.0, jnp.float32)
        best_ref[...] = jnp.full(best_ref.shape, -1.0, jnp.float32)

    left, right = first[step], second[step]
    i = lax.broadcasted_iota(jnp.int32, (width, width), 0)
    j = lax.broadcasted_iota(jnp.int32, (width, width), 1)
    rows = unit_ref[pl.ds(pl.multiple_of(left * 256, 256), 256), :]
    cols = unit_ref[pl.ds(pl.multiple_of(right * 256, 256), 256), :]
    scores = lax.dot_general(rows, cols, (((1,), (1,)), ((), ())), preferred_element_type=jnp.float32)
    for a in range(2):
        for b in range(2):
            r, c = left * 2 + a, right * 2 + b
            limit = jnp.where(linked[r * blocks + c] > 0, counts[r], 0)
            keep = (i < limit) & (j < counts[c]) & ((r != c) | (i != j))
            part = jnp.where(keep, scores[a * width : (a + 1) * width, b * width : (b + 1) * width], -1.0)
            held[r] = jnp.maximum(held[r], part)
            best_ref[pl.ds(c, 1), :] = jnp.maximum(best_ref[pl.ds(c, 1), :], jnp.max(part, axis=0, keepdims=True))

    @pl.when(step == pl.num_programs(0) - 1)
    def _():
        for b in range(blocks):
            best_ref[pl.ds(b, 1), :] = jnp.maximum(
                best_ref[pl.ds(b, 1), :], jnp.max(held[b].T, axis=0, keepdims=True)
            )


def nearby_maxima(unit, counts, linked):
    rows, depth = unit.shape
    blocks = counts.shape[0]
    sides = rows // 256
    first, second = np.triu_indices(sides)
    return pl.pallas_call(
        nearby_kernel,
        grid_spec=pltpu.PrefetchScalarGridSpec(
            num_scalar_prefetch=4,
            grid=(len(first),),
            in_specs=[pl.BlockSpec((rows, depth), lambda i, *_: (0, 0))],
            out_specs=pl.BlockSpec((blocks, rows // blocks), lambda i, *_: (0, 0)),
            scratch_shapes=[pltpu.VMEM((blocks, 128, 128), jnp.float32)],
        ),
        out_shape=jax.ShapeDtypeStruct((blocks, rows // blocks), jnp.float32),
        compiler_params=pltpu.CompilerParams(vmem_limit_bytes=16 * MIB),
        cost_estimate=pl.CostEstimate(
            flops=2 * len(first) * 256 * 256 * depth, bytes_accessed=2 * rows * depth, transcendentals=0
        ),
        name="nearby",
    )(
        jnp.asarray(first, jnp.int32),
        jnp.asarray(second, jnp.int32),
        linked,
        counts,
        unit,
    )


def exact_dot(a, b):
    return jnp.dot(
        a.astype(jnp.float32).astype(jnp.bfloat16),
        b.astype(jnp.float32).astype(jnp.bfloat16),
        preferred_element_type=jnp.float32,
    ).astype(jnp.int32)


def flip(a):
    return a.astype(jnp.float32).T.astype(jnp.int32)


def plan_kernel(
    direct, items, relayed, chips, me_ref, pair_ref, count_ref, count_t_ref,
    send_ref, far_ref, code_ref, far_code_ref, hand_ref, target_ref, back_ref, fits_ref,
    w_lo, w_hi, sums, mine,
):
    device = me_ref[0]
    chip, core = device // 2, device % 2
    devices = 2 * chips
    flat = (chips, chips)
    pair = pair_ref[...]
    code = jnp.maximum(pair, 0)
    row_of, col_of = code >> 4, code & 15
    row_count = jnp.zeros(pair.shape, jnp.int32)
    col_count = jnp.zeros(pair.shape, jnp.int32)
    for l in range(16):
        row_count = jnp.where(row_of == l, count_t_ref[pl.ds(l, 1), :], row_count)
        col_count = jnp.where(col_of == l, count_ref[:, l : l + 1], col_count)

    xs = lax.broadcasted_iota(jnp.int32, (chips, devices), 0)
    ds = lax.broadcasted_iota(jnp.int32, (chips, devices), 1)
    pick = [(ds == 2 * xs + i).astype(jnp.int32) for i in range(2)]
    pick_t = [flip(p) for p in pick]

    def split(values):
        half = [exact_dot(p, values) for p in pick]
        return [[exact_dot(half[i], pick_t[j]) for j in range(2)] for i in range(2)]

    asked = {"code": split(pair + 1), "row": split(row_count), "col": split(col_count)}
    asked_t = {k: [[flip(v[j][i]) for j in range(2)] for i in range(2)] for k, v in asked.items()}

    x = lax.broadcasted_iota(jnp.int32, flat, 0)
    y = lax.broadcasted_iota(jnp.int32, flat, 1)
    low, same = x <= y, x == y
    edges = []
    for kind in range(2):
        for p in range(2):
            for q in range(2):
                first, second = (asked_t, asked) if kind == 0 else (asked, asked_t)
                here = {k: jnp.where(low, first[k][p][q], second[k][q][p]) for k in asked}
                exists = here["code"] > 0
                if kind == 1:
                    exists = exists & ~same
                number = jnp.maximum(here["code"] - 1, 0)
                r, c = number >> 4, number & 15
                side = jnp.where(low, p, q) * 16
                other = jnp.where(low, q, p) * 16
                owns_row = low if kind == 0 else ~low
                own_block = side + jnp.where(owns_row, r, c)
                other_block = other + jnp.where(owns_row, c, r)
                own_rows = jnp.where(exists, jnp.where(owns_row, here["row"], here["col"]), 0)
                other_rows = jnp.where(exists, jnp.where(owns_row, here["col"], here["row"]), 0)
                edges.append((exists, own_block, other_block, own_rows, other_rows))
    for e, (exists, _, _, own_rows, other_rows) in enumerate(edges):
        own_units, other_units = (own_rows + 15) >> 4, (other_rows + 15) >> 4
        w_lo[e] = jnp.where(low, own_units, other_units)
        w_hi[e] = jnp.where(low, other_units, own_units)

    for half in range(2):
        for choice in range(16):
            up = jnp.zeros(flat, jnp.int32)
            down = jnp.zeros(flat, jnp.int32)
            for b in range(4):
                if choice >> b & 1:
                    up = up + w_lo[half * 4 + b]
                else:
                    down = down + w_hi[half * 4 + b]
            lanes = pl.ds(0, chips) if half or choice < 8 else pl.ds(chips, chips)
            spot = choice if half else choice % 8
            sums[half, spot, :, lanes] = up
            sums[2 + half, spot, :, lanes] = down
            if half:
                sums[1, spot, :, pl.ds(chips, chips)] = up
                sums[3, spot, :, pl.ds(chips, chips)] = down
    eight = jnp.where(lax.broadcasted_iota(jnp.int32, (chips, devices), 1) < chips, 0, 8)

    def try_half(a, least):
        up_a, down_a = sums[0, a] - 2 * direct, sums[2, a] - 2 * direct
        for b in range(16):
            up, down = up_a + sums[1, b], down_a + sums[3, b]
            over = jnp.maximum(up, 0) + jnp.maximum(down, 0)
            rank = over * 65536 + jnp.maximum(up, down) * 256 + (b * 16 + a) + eight
            least = jnp.minimum(least, rank)
        return least

    least = lax.fori_loop(0, 8, try_half, jnp.full((chips, devices), 2**30, jnp.int32))
    least = jnp.minimum(least[:, :chips], least[:, chips:])
    chosen = jnp.where(same, 255, least & 255)

    out_total = jnp.zeros(flat, jnp.int32)
    in_total = jnp.zeros(flat, jnp.int32)
    for e, (exists, own_block, other_block, own_rows, other_rows) in enumerate(edges):
        bit = (chosen >> e) & 1
        sends = exists & ((bit == 1) == low)
        out_units = jnp.where(sends, (own_rows + 15) >> 4, 0)
        in_rows = jnp.where(same, own_rows, other_rows)
        in_units = jnp.where((exists & ~sends) | same, (in_rows + 15) >> 4, 0)
        out_total = out_total + out_units
        in_total = in_total + in_units
        mine[e] = out_units
        mine[8 + e] = own_block ^ (core * 16)
        mine[16 + e] = in_units
        mine[24 + e] = jnp.where(same, other_block, own_block) ^ (core * 16)
        mine[32 + e] = in_rows
    mine[40] = out_total
    mine[41] = in_total

    far = jnp.maximum(out_total - 2 * direct, 0)
    before = exact_dot(far, (x < y).astype(jnp.int32))
    total = jnp.sum(far, axis=1, keepdims=True)
    at_self = jnp.sum(jnp.where(same, before, 0), axis=1, keepdims=True)
    rank = before - at_self + jnp.where(y < x, total, 0)
    over_out = jnp.max((total + COLORS - 1) >> LOG_COLORS)
    over_in = jnp.zeros((), jnp.int32)
    earlier = (y < x).astype(jnp.int32)
    number, place, first = [], [], []
    for color in range(COLORS):
        first.append((color - rank) & (COLORS - 1))
        number.append((far - first[-1] + COLORS - 1) >> LOG_COLORS)
        over_in = jnp.maximum(over_in, jnp.max(jnp.sum(number[-1], axis=0, keepdims=True)))
        place.append(exact_dot(earlier, number[-1]))
    room = turns(direct)
    fits = (over_out <= items) & (over_in <= relayed) & (jnp.max(far) <= room * COLORS)
    fits_ref[0] = fits.astype(jnp.int32)
    odd = core == 1
    own_class = chip // (chips // CLASSES)
    hand_number = jnp.zeros(flat, jnp.int32)
    hand_place = jnp.zeros(flat, jnp.int32)
    hand_first = jnp.zeros(flat, jnp.int32)
    for k in range(CLASSES):
        picked = [jnp.where(odd, v[2 * k + 1], v[2 * k]) for v in (number, place, first)]
        for n, v in enumerate(picked):
            mine[44 + 6 * k + n] = v
            mine[47 + 6 * k + n] = flip(v)
        here = own_class == k
        hand_number = jnp.where(here, picked[0], hand_number)
        hand_place = jnp.where(here, picked[1], hand_place)
        hand_first = jnp.where(here, picked[2], hand_first)
    mine[42] = rank
    mine[43] = far
    own = pl.ds(chip, 1)

    out_units = [mine[e, own, :] for e in range(SHARE)]
    out_block = [mine[8 + e, own, :] for e in range(SHARE)]
    in_units = [mine[16 + e, own, :] for e in range(SHARE)]
    in_block = [mine[24 + e, own, :] for e in range(SHARE)]
    in_rows = [mine[32 + e, own, :] for e in range(SHARE)]
    out_total, in_total, rank_own, far_own = (mine[40 + k, own, :] for k in range(4))

    def lane(total):
        plain = jnp.minimum(total, 2 * direct)
        half = (plain + 1) >> 1
        return jnp.where(odd, half, 0), jnp.where(odd, plain - half, half)

    def unit_at(position, valid):
        value = jnp.full(position.shape, -1, jnp.int32)
        start = jnp.zeros((1, chips), jnp.int32)
        for e in range(SHARE):
            hit = valid & (position >= start) & (position < start + out_units[e])
            value = jnp.where(hit, out_block[e] * 8 + position - start, value)
            start = start + out_units[e]
        return value

    def code_at(position, valid):
        value = jnp.zeros(position.shape, jnp.int32)
        start = jnp.zeros((1, chips), jnp.int32)
        for e in range(SHARE):
            hit = valid & (position >= start) & (position < start + in_units[e])
            rows = jnp.minimum(in_rows[e] - UNIT * (position - start), UNIT)
            value = jnp.where(hit, in_block[e] * 32 + 32 + rows, value)
            start = start + in_units[e]
        return value

    step = lax.broadcasted_iota(jnp.int32, (direct, chips), 0)
    begin, length = lane(out_total)
    plain = unit_at(begin + step, step < length)
    send_ref[...] = jnp.maximum(plain, 0)
    target_ref[pl.ds(0, direct), :] = plain
    begin, length = lane(in_total)
    code_ref[...] = code_at(begin + step, step < length)

    if items:
        slot = lax.broadcasted_iota(jnp.int32, (items, chips), 0)
        place_in = lax.broadcasted_iota(jnp.int32, (relayed, chips), 0)
        for k in range(CLASSES):
            turn = COLORS * slot + 2 * k + core - rank_own
            unit = unit_at(2 * direct + turn, (turn >= 0) & (turn < far_own))
            far_ref[:, k : k + 1] = jnp.sum(jnp.maximum(unit, 0), axis=1, keepdims=True)
            number, place, first, number_t, place_t, first_t = (mine[44 + 6 * k + n, own, :] for n in range(6))
            made = jnp.zeros((relayed, chips), jnp.int32)
            for n in range(room):
                target_ref[pl.ds(direct + CLASSES * n + k, 1), :] = unit_at(
                    2 * direct + first + COLORS * n, n < number
                )
                back_ref[pl.ds(CLASSES * n + k, 1), :] = jnp.where(n < number_t, place_t + n, -1)
                hit = (place_t + n == place_in) & (n < number_t)
                made = made + code_at(2 * direct + first_t + COLORS * n + 0 * place_in, hit)
            far_code_ref[:, k : k + 1] = jnp.sum(made, axis=1, keepdims=True)
        hand_number, hand_place, hand_from = (
            flip(hand_number), flip(hand_place), flip((rank + hand_first) >> LOG_COLORS)
        )
        for q in range(relayed):
            value = jnp.zeros(flat, jnp.int32)
            for n in range(room):
                hit = (hand_place + n == q) & (n < hand_number)
                value = value + jnp.where(hit, y * items + hand_from + n, 0)
            hand_ref[:, q : q + 1] = jnp.sum(value, axis=1, keepdims=True)


def make_plan(direct, items, relayed, told, device):
    devices, columns = told.shape
    chips = devices // 2
    ints = lambda *shape: jax.ShapeDtypeStruct(shape, jnp.int32)
    vmem = pl.BlockSpec(memory_space=pltpu.VMEM)
    return pl.pallas_call(
        functools.partial(plan_kernel, direct, items, relayed, chips),
        in_specs=[pl.BlockSpec(memory_space=pltpu.SMEM), vmem, vmem, vmem],
        out_specs=[vmem] * 7 + [pl.BlockSpec(memory_space=pltpu.SMEM)],
        out_shape=[
            ints(direct, chips),
            ints(max(items, 8), CLASSES),
            ints(direct, chips),
            ints(max(relayed, 8), CLASSES),
            ints(chips, max(relayed, 8)),
            ints(direct + turns(direct) * CLASSES, chips),
            ints(max(turns(direct), 1) * CLASSES, chips),
            ints(1),
        ],
        scratch_shapes=[
            pltpu.VMEM((SHARE, chips, chips), jnp.int32),
            pltpu.VMEM((SHARE, chips, chips), jnp.int32),
            pltpu.VMEM((4, 16, chips, devices), jnp.int32),
            pltpu.VMEM((44 + 6 * CLASSES, chips, chips), jnp.int32),
        ],
        compiler_params=pltpu.CompilerParams(vmem_limit_bytes=32 * MIB),
        cost_estimate=pl.CostEstimate(flops=10**11, bytes_accessed=10**6, transcendentals=0),
        name="plan",
    )(device.reshape(1), told[:, :devices], told[:, devices:], told[:, devices:].T)


def turn(first, second, values):
    rows = first * second
    o = lax.broadcasted_iota(jnp.int32, (rows, rows), 0)
    i = lax.broadcasted_iota(jnp.int32, (rows, rows), 1)
    take = ((o % first) * second + o // first == i).astype(jnp.float32).astype(jnp.bfloat16)
    return jnp.dot(take, values, preferred_element_type=jnp.float32).astype(jnp.bfloat16)


def fetch(near_ref, far_ref, held, sems):
    half = near_ref.shape[0]
    copies = [
        pltpu.make_async_copy(near_ref, held.at[pl.ds(0, half)], sems.at[0]),
        pltpu.make_async_copy(far_ref, held.at[pl.ds(half, half)], sems.at[1]),
    ]
    for copy in copies:
        copy.start()
    for copy in copies:
        copy.wait()


def pack_kernel(group, direct, items, send, far, near_ref, far_ref, out_ref, held, gathered, turned, sems):
    step = pl.program_id(0)
    chips = pl.num_programs(0) * group

    @pl.when(step == 0)
    def _():
        fetch(near_ref, far_ref, held, sems)
        if items:
            for p in range(CLASSES):
                for q in range(items):
                    gathered[pl.ds(q * UNIT, UNIT), :] = held[far[q * CLASSES + p]]
                size = items * UNIT
                turned[pl.ds(p * size, size), :] = turn(items, UNIT, gathered[...])

    for k in range(group):
        slot = step * group + k
        for p in range(direct):
            out_ref[k, pl.ds(p * UNIT, UNIT), :] = held[send[p * chips + slot]]
        if items:
            out_ref[k, pl.ds(direct * UNIT, items), :] = turned[pl.ds(pl.multiple_of(slot * items, items), items), :]


def pack(direct, items, send, far, near_units, far_units):
    units, _, depth = near_units.shape
    chips = send.shape[1]
    rows = direct * UNIT + items
    group = 4
    some = max(items, 16)
    return pl.pallas_call(
        functools.partial(pack_kernel, group, direct, items),
        grid_spec=pltpu.PrefetchScalarGridSpec(
            num_scalar_prefetch=2,
            grid=(chips // group,),
            in_specs=[pl.BlockSpec(memory_space=pl.ANY)] * 2,
            out_specs=pl.BlockSpec((group, rows, depth), lambda i, *_: (i, 0, 0)),
            scratch_shapes=[
                pltpu.VMEM((2 * units, UNIT, depth), jnp.bfloat16),
                pltpu.VMEM((some * UNIT, depth), jnp.bfloat16),
                pltpu.VMEM((some * chips, depth), jnp.bfloat16),
                pltpu.SemaphoreType.DMA((2,)),
            ],
        ),
        out_shape=jax.ShapeDtypeStruct((chips, rows, depth), jnp.bfloat16),
        compiler_params=pltpu.CompilerParams(vmem_limit_bytes=20 * MIB),
        name="pack",
    )(send.reshape(-1), far.reshape(-1), near_units, far_units)


def relay_kernel(hand_ref, held_ref, target_ref, back_ref, out_ref, target_out, back_out):
    target_out[...] = target_ref[...]
    back_out[...] = back_ref[...]
    held = held_ref[...]
    rows = held.shape[0] * held.shape[1]
    i = lax.broadcasted_iota(jnp.int32, (out_ref.shape[0], rows), 1)
    take = (hand_ref[...] == i).astype(jnp.float32).astype(jnp.bfloat16)
    out_ref[...] = jnp.dot(
        take, held.reshape(rows, held.shape[2]), preferred_element_type=jnp.float32
    ).astype(jnp.bfloat16)


def relay(hand, arrived, target, back, direct, items):
    chips, relayed = hand.shape
    depth = arrived.shape[2]
    step = 256
    tables = [pl.BlockSpec(t.shape, lambda i: (0, 0)) for t in (target, back)]
    passed, target, back = pl.pallas_call(
        relay_kernel,
        grid=(chips * relayed // step,),
        in_specs=[
            pl.BlockSpec((step, 1), lambda i: (i, 0)),
            pl.BlockSpec((chips, items, depth), lambda i: (0, direct * UNIT // items, 0)),
            *tables,
        ],
        out_specs=[pl.BlockSpec((step, depth), lambda i: (i, 0)), *tables],
        out_shape=[
            jax.ShapeDtypeStruct((chips * relayed, depth), jnp.bfloat16),
            jax.ShapeDtypeStruct(target.shape, jnp.int32),
            jax.ShapeDtypeStruct(back.shape, jnp.int32),
        ],
        compiler_params=pltpu.CompilerParams(vmem_limit_bytes=54 * MIB),
        name="relay",
    )(hand.reshape(-1, 1), arrived, target, back)
    return passed.reshape(chips, relayed, depth), target, back


def score_kernel(
    places, group, turned, codes, counts, near_ref, far_ref, arrived_ref, back_ref, best_ref,
    held, rows_held, batch, tiles, head, follow, sems,
):
    slots = back_ref.shape[0]
    blocks, width, _ = held.shape
    copies = [
        pltpu.make_async_copy(near_ref, held.at[pl.ds(0, blocks // 2)], sems.at[0]),
        pltpu.make_async_copy(far_ref, held.at[pl.ds(blocks // 2, blocks // 2)], sems.at[1]),
    ]
    if turned:
        copies.append(pltpu.make_async_copy(arrived_ref, rows_held, sems.at[2]))
    else:
        copies.append(pltpu.make_async_copy(arrived_ref.at[:, pl.ds(0, places * UNIT)], rows_held, sems.at[2]))
    for copy in copies:
        copy.start()
    best_ref[...] = jnp.full(best_ref.shape, -1.0, jnp.float32)
    tiles[...] = jnp.full(tiles.shape, -1.0, jnp.float32)

    def clear(b, carry):
        head[b] = -1
        return carry

    lax.fori_loop(0, blocks, clear, 0)

    def link(slot, carry):
        for p in range(places):
            made = codes[p * slots + slot]
            block = jnp.maximum((made >> 5) - 1, 0)
            unit = slot * 32 + p

            @pl.when(made > 0)
            def _():
                follow[unit] = head[block]
                head[block] = unit

        return carry

    lax.fori_loop(0, slots, link, 0)
    for copy in copies:
        copy.wait()
    if turned:
        for slot in range(slots):
            rows_held[slot] = turn(UNIT, places, rows_held[slot])

    i = lax.broadcasted_iota(jnp.int32, (UNIT, width), 0)
    j = lax.broadcasted_iota(jnp.int32, (UNIT, width), 1)

    def per_block(block, carry):
        columns = j < counts[block]

        def some_units(unit):
            taken = []
            for g in range(group):
                live = unit >= 0
                here = jnp.maximum(unit, 0)
                slot, p = here >> 5, here & 31
                batch[pl.ds(g * UNIT, UNIT), :] = rows_held[slot, pl.ds(pl.multiple_of(p * UNIT, UNIT), UNIT), :]
                rows = jnp.where(live, codes[p * slots + slot] & 31, 0)
                taken.append((jnp.where(live, slot, slots), p, rows))
                unit = jnp.where(live, follow[here], -1)
            scores = lax.dot_general(
                batch[...], held[block], (((1,), (1,)), ((), ())), preferred_element_type=jnp.float32
            )
            most = best_ref[pl.ds(block, 1), :]
            for g, (slot, p, rows) in enumerate(taken):
                tile = jnp.where((i < rows) & columns, scores[g * UNIT : (g + 1) * UNIT], -1.0)
                tiles[slot, pl.ds(pl.multiple_of(p * UNIT, UNIT), UNIT), :] = tile
                most = jnp.maximum(most, jnp.max(tile, axis=0, keepdims=True))
            best_ref[pl.ds(block, 1), :] = most
            return unit

        lax.while_loop(lambda unit: unit >= 0, some_units, head[block])
        return carry

    lax.fori_loop(0, blocks, per_block, 0)

    if slots % 8 == 0:

        def finish(part, carry):
            for k in range(8):
                slot = part * 8 + k
                back_ref[pl.ds(slot, 1), :] = jnp.max(tiles[slot].T, axis=0, keepdims=True)
            return carry

        lax.fori_loop(0, slots // 8, finish, 0)
    else:
        for slot in range(slots):
            back_ref[slot : slot + 1, :] = jnp.max(tiles[slot].T, axis=0, keepdims=True)


def score(codes, counts, near, far, arrived, group, turned):
    blocks, width, depth = near.shape
    places, slots = codes.shape
    rows = places * UNIT
    any_place = pl.BlockSpec(memory_space=pl.ANY)
    vmem = pl.BlockSpec(memory_space=pltpu.VMEM)
    smem = pl.BlockSpec(memory_space=pltpu.SMEM)
    return pl.pallas_call(
        functools.partial(score_kernel, places, group, turned),
        in_specs=[smem, smem, any_place, any_place, any_place],
        out_specs=[vmem, vmem],
        out_shape=[
            jax.ShapeDtypeStruct((slots, rows), jnp.float32),
            jax.ShapeDtypeStruct((2 * blocks, width), jnp.float32),
        ],
        scratch_shapes=[
            pltpu.VMEM((2 * blocks, width, depth), jnp.bfloat16),
            pltpu.VMEM((slots, rows, depth), jnp.bfloat16),
            pltpu.VMEM((group * UNIT, depth), jnp.bfloat16),
            pltpu.VMEM((slots + 1, rows, width), jnp.float32),
            pltpu.SMEM((2 * blocks,), jnp.int32),
            pltpu.SMEM((slots * 32,), jnp.int32),
            pltpu.SemaphoreType.DMA((3,)),
        ],
        compiler_params=pltpu.CompilerParams(vmem_limit_bytes=56 * MIB),
        cost_estimate=pl.CostEstimate(
            flops=2 * slots * rows * width * depth, bytes_accessed=2 * slots * rows * depth, transcendentals=0
        ),
        name="score",
    )(codes.reshape(-1), counts, near, far, arrived)


def one_hot(index, count, valid):
    return (index[:, None] == jnp.arange(count, dtype=jnp.int32)[None, :]) & valid[:, None]


def exchange(values, chips):
    groups = [[2 * x + c for x in range(chips)] for c in range(2)]
    return lax.all_to_all(values, "shard", split_axis=0, concat_axis=0, axis_index_groups=groups, tiled=True)


def far_maxima(direct, items, relayed, plan, counts, linked, near, far):
    send, own_far, codes, far_codes, hand, target, item_back, _ = plan
    blocks, width, depth = near.shape
    chips = send.shape[1]
    outgoing = pack(
        direct, items, send, own_far,
        near.reshape(-1, UNIT, depth), far.reshape(-1, UNIT, depth),
    )
    arrived = exchange(outgoing, chips)
    arrived, near, far, counts, linked, codes, far_codes, hand, target, item_back = lax.optimization_barrier(
        (arrived, near, far, counts, linked, codes, far_codes, hand, target, item_back)
    )
    if items:
        passed, target, item_back = relay(hand, arrived, target, item_back, direct, items)
        gained = exchange(passed, chips)
    back, best = score(codes, counts, near, far, arrived, 16, False)
    best = jnp.concatenate(
        [jnp.maximum(best[:blocks], nearby_maxima(near.reshape(-1, depth), counts[:blocks], linked)), best[blocks:]]
    )
    places = direct
    if items:
        gained = gained.reshape(CLASSES, chips // CLASSES * relayed, depth)
        far_back, far_best = score(far_codes, counts, near, far, gained, 4, True)
        best = jnp.maximum(best, far_best)
        hit = item_back.reshape(turns(direct), CLASSES, chips)[..., None] == jnp.arange(relayed, dtype=jnp.int32)
        far_back = far_back.reshape(1, CLASSES, 1, relayed, UNIT)
        far_back = jnp.where(hit[..., None], far_back, -1.0).max(axis=3)
        far_back = far_back.transpose(2, 0, 1, 3).reshape(chips, -1)
        back = jnp.concatenate([back, far_back], axis=1)
        places = direct + turns(direct) * CLASSES
    returned = exchange(back, chips).reshape(chips, places, UNIT)
    spots = target[:places].T.reshape(-1)
    values = returned.reshape(-1, UNIT).T
    number = 2 * blocks * width // UNIT
    hit = spots[:, None] == jnp.arange(number, dtype=jnp.int32)[None, :]
    folded = jnp.where(hit[None], values[:, :, None], -1.0).max(axis=1)
    return jnp.maximum(best, folded.T.reshape(2 * blocks, width))


def on_device(embeddings, block_rows, pairs):
    blocks = block_rows.shape[0]
    width = embeddings.shape[0] // blocks
    peers = lax.axis_size("shard")
    myself = lax.axis_index("shard")
    swap = [(d, d ^ 1) for d in range(peers)]
    row_block, col_block = pairs[:, 0], pairs[:, 1]
    alive = pairs[:, 2] == myself
    owner = row_block // blocks
    remote = alive & (owner != myself)
    row_local, col_local = row_block % blocks, col_block % blocks
    tell = ask(myself, pairs, block_rows, peers)
    told = lax.all_to_all(tell, "shard", split_axis=0, concat_axis=0, tiled=True)[:, 0]

    unit = normalize(embeddings, tell)
    near = unit.reshape(blocks, width, -1)
    far = lax.ppermute(near, "shard", swap)

    nearby = alive & ~remote
    row_table = one_hot(row_local, blocks, nearby).astype(jnp.float32)
    col_table = one_hot(col_local, blocks, nearby).astype(jnp.float32)
    adjacency = (
        lax.dot_general(row_table, col_table, (((0,), (0,)), ((), ())), preferred_element_type=jnp.float32) > 0.5
    )
    linked = (adjacency | adjacency.T).astype(jnp.int32).reshape(-1)

    plan = make_plan(*PLANS[0], told, myself)
    counts = jnp.concatenate([block_rows, lax.dynamic_slice_in_dim(told, myself ^ 1, 1, 0)[0, peers:]])

    def attempt(level, plan):
        def here():
            return far_maxima(*PLANS[level], plan, counts, linked, near, far)

        def later():
            return attempt(level + 1, make_plan(*PLANS[level + 1], told, myself))

        return lax.cond(plan[-1][0] > 0, here, later) if level + 1 < len(PLANS) else here()

    both = attempt(0, plan)
    other = lax.ppermute(both[blocks:], "shard", swap)
    return jnp.maximum(both[:blocks], other)


def solution(mesh):
    placed = (P("shard", None), P("shard"), P("shard", None))
    return jax.shard_map(
        on_device, mesh=mesh, in_specs=placed, out_specs=P("shard", None), check_vma=False
    )
```

```python
import functools

import jax
import jax.numpy as jnp
import numpy as np
from jax import lax
from jax.experimental import pallas as pl
from jax.experimental.pallas import tpu as pltpu
from jax.sharding import PartitionSpec as P

UNIT = 16
CLASSES = 4
COLORS = 2 * CLASSES
LOG_COLORS = 3
PLANS = ((7, 16, 24), (8, 16, 16), (16, 0, 0))
SHARE = 8
MIB = 1024 * 1024


def turns(direct):
    return -(-(2 * 16 - 2 * direct) // COLORS)


def ask_kernel(me_ref, pairs_ref, rows_ref, tell_ref):
    device = me_ref[0]
    peers, _, columns = tell_ref.shape
    row, col = pairs_ref[0:1, :], pairs_ref[1:2, :]
    owner = row >> 4
    far = (pairs_ref[2:3, :] == device) & (owner != device)
    peer = lax.broadcasted_iota(jnp.int32, (peers, row.shape[1]), 0)
    code = (row & 15) * 16 + (col & 15)
    code = jnp.where((owner == peer) & far, code, -1).astype(jnp.float32)
    most = code[:, :peers]
    for k in range(1, row.shape[1] // peers):
        most = jnp.maximum(most, code[:, k * peers : (k + 1) * peers])
    wanted = jnp.max(most.T, axis=0, keepdims=True).astype(jnp.int32)
    tell = jnp.concatenate([wanted, rows_ref[...]], axis=1)
    tell_ref[...] = jnp.broadcast_to(tell[None], tell_ref.shape)


def ask(device, pairs, block_rows, peers):
    blocks = block_rows.shape[0]
    assert blocks == 16
    vmem = pl.BlockSpec(memory_space=pltpu.VMEM)
    return pl.pallas_call(
        ask_kernel,
        in_specs=[pl.BlockSpec(memory_space=pltpu.SMEM), vmem, vmem],
        out_specs=vmem,
        out_shape=jax.ShapeDtypeStruct((peers, 1, peers + blocks), jnp.int32),
        name="ask",
    )(device.reshape(1), pairs.T, block_rows.reshape(1, blocks))


def normalize_kernel(after_ref, values_ref, unit_ref):
    values = values_ref[...].astype(jnp.float32)
    total = jnp.sum(values * values, axis=-1, keepdims=True)
    unit_ref[...] = (values * lax.rsqrt(total + 1e-06)).astype(jnp.bfloat16)


def normalize(embeddings, after):
    rows, depth = embeddings.shape
    step = 512
    return pl.pallas_call(
        normalize_kernel,
        grid=(rows // step,),
        in_specs=[pl.BlockSpec(memory_space=pl.ANY), pl.BlockSpec((step, depth), lambda i: (i, 0))],
        out_specs=pl.BlockSpec((step, depth), lambda i: (i, 0)),
        out_shape=jax.ShapeDtypeStruct((rows, depth), jnp.bfloat16),
        cost_estimate=pl.CostEstimate(flops=4 * rows * depth, bytes_accessed=4 * rows * depth, transcendentals=rows),
        name="normalize",
    )(after, embeddings)


def near_pairs(blocks):
    return np.array([(i, j) for i in range(blocks // 4) for j in range(blocks // 2) if (j + 1) * 2 > i * 4], np.int32)


def score_near(near, linked, counts, rows_ref, best_ref, kept):
    blocks, width, depth = rows_ref.shape[0] // 2, rows_ref.shape[1], rows_ref.shape[2]
    kept[...] = jnp.full(kept.shape, -1.0, jnp.float32)
    i = lax.broadcasted_iota(jnp.int32, (width, width), 0)
    j = lax.broadcasted_iota(jnp.int32, (width, width), 1)

    def step(number, carry):
        left, right = near[2 * number], near[2 * number + 1]
        rows = rows_ref[pl.ds(left * 4, 4)].reshape(4 * width, depth)
        cols = rows_ref[pl.ds(right * 2, 2)].reshape(2 * width, depth)
        scores = lax.dot_general(rows, cols, (((1,), (1,)), ((), ())), preferred_element_type=jnp.float32)
        for b in range(2):
            c = right * 2 + b
            most = best_ref[pl.ds(c, 1), :]
            for a in range(4):
                r = left * 4 + a
                limit = jnp.where(linked[r * blocks + c] > 0, counts[r], 0)
                keep = (i < limit) & (j < counts[c]) & ((r != c) | (i != j))
                part = jnp.where(keep, scores[a * width : (a + 1) * width, b * width : (b + 1) * width], -1.0)
                kept[r] = jnp.maximum(kept[r], part)
                most = jnp.maximum(most, jnp.max(part, axis=0, keepdims=True))
            best_ref[pl.ds(c, 1), :] = most
        return carry

    lax.fori_loop(0, len(near_pairs(blocks)), step, 0)
    for b in range(blocks):
        best_ref[pl.ds(b, 1), :] = jnp.maximum(best_ref[pl.ds(b, 1), :], jnp.max(kept[b].T, axis=0, keepdims=True))


def exact_dot(a, b):
    return jnp.dot(
        a.astype(jnp.float32).astype(jnp.bfloat16),
        b.astype(jnp.float32).astype(jnp.bfloat16),
        preferred_element_type=jnp.float32,
    ).astype(jnp.int32)


def flip(a):
    return a.astype(jnp.float32).T.astype(jnp.int32)


def plan_kernel(
    direct, items, relayed, chips, me_ref, pair_ref, count_ref, count_t_ref,
    send_ref, far_ref, code_ref, far_code_ref, hand_ref, target_ref, back_ref, fits_ref,
    w_lo, w_hi, sums, mine,
):
    device = me_ref[0]
    chip, core = device // 2, device % 2
    devices = 2 * chips
    flat = (chips, chips)
    pair = pair_ref[...]
    code = jnp.maximum(pair, 0)
    row_of, col_of = code >> 4, code & 15
    row_count = jnp.zeros(pair.shape, jnp.int32)
    col_count = jnp.zeros(pair.shape, jnp.int32)
    for l in range(16):
        row_count = jnp.where(row_of == l, count_t_ref[pl.ds(l, 1), :], row_count)
        col_count = jnp.where(col_of == l, count_ref[:, l : l + 1], col_count)

    xs = lax.broadcasted_iota(jnp.int32, (chips, devices), 0)
    ds = lax.broadcasted_iota(jnp.int32, (chips, devices), 1)
    pick = [(ds == 2 * xs + i).astype(jnp.int32) for i in range(2)]
    pick_t = [flip(p) for p in pick]

    def split(values):
        half = [exact_dot(p, values) for p in pick]
        return [[exact_dot(half[i], pick_t[j]) for j in range(2)] for i in range(2)]

    asked = {"code": split(pair + 1), "row": split(row_count), "col": split(col_count)}
    asked_t = {k: [[flip(v[j][i]) for j in range(2)] for i in range(2)] for k, v in asked.items()}

    x = lax.broadcasted_iota(jnp.int32, flat, 0)
    y = lax.broadcasted_iota(jnp.int32, flat, 1)
    low, same = x <= y, x == y
    edges = []
    for kind in range(2):
        for p in range(2):
            for q in range(2):
                first, second = (asked_t, asked) if kind == 0 else (asked, asked_t)
                here = {k: jnp.where(low, first[k][p][q], second[k][q][p]) for k in asked}
                exists = here["code"] > 0
                if kind == 1:
                    exists = exists & ~same
                number = jnp.maximum(here["code"] - 1, 0)
                r, c = number >> 4, number & 15
                side = jnp.where(low, p, q) * 16
                other = jnp.where(low, q, p) * 16
                owns_row = low if kind == 0 else ~low
                own_block = side + jnp.where(owns_row, r, c)
                other_block = other + jnp.where(owns_row, c, r)
                own_rows = jnp.where(exists, jnp.where(owns_row, here["row"], here["col"]), 0)
                other_rows = jnp.where(exists, jnp.where(owns_row, here["col"], here["row"]), 0)
                edges.append((exists, own_block, other_block, own_rows, other_rows))
    for e, (exists, _, _, own_rows, other_rows) in enumerate(edges):
        own_units, other_units = (own_rows + 15) >> 4, (other_rows + 15) >> 4
        w_lo[e] = jnp.where(low, own_units, other_units)
        w_hi[e] = jnp.where(low, other_units, own_units)

    for half in range(2):
        for choice in range(16):
            up = jnp.zeros(flat, jnp.int32)
            down = jnp.zeros(flat, jnp.int32)
            for b in range(4):
                if choice >> b & 1:
                    up = up + w_lo[half * 4 + b]
                else:
                    down = down + w_hi[half * 4 + b]
            lanes = pl.ds(0, chips) if half or choice < 8 else pl.ds(chips, chips)
            spot = choice if half else choice % 8
            sums[half, spot, :, lanes] = up
            sums[2 + half, spot, :, lanes] = down
            if half:
                sums[1, spot, :, pl.ds(chips, chips)] = up
                sums[3, spot, :, pl.ds(chips, chips)] = down
    eight = jnp.where(lax.broadcasted_iota(jnp.int32, (chips, devices), 1) < chips, 0, 8)

    def try_half(a, least):
        up_a, down_a = sums[0, a] - 2 * direct, sums[2, a] - 2 * direct
        for b in range(16):
            up, down = up_a + sums[1, b], down_a + sums[3, b]
            over = jnp.maximum(up, 0) + jnp.maximum(down, 0)
            rank = over * 65536 + jnp.maximum(up, down) * 256 + (b * 16 + a) + eight
            least = jnp.minimum(least, rank)
        return least

    least = lax.fori_loop(0, 8, try_half, jnp.full((chips, devices), 2**30, jnp.int32))
    least = jnp.minimum(least[:, :chips], least[:, chips:])
    chosen = jnp.where(same, 255, least & 255)

    out_total = jnp.zeros(flat, jnp.int32)
    in_total = jnp.zeros(flat, jnp.int32)
    for e, (exists, own_block, other_block, own_rows, other_rows) in enumerate(edges):
        bit = (chosen >> e) & 1
        sends = exists & ((bit == 1) == low)
        out_units = jnp.where(sends, (own_rows + 15) >> 4, 0)
        in_rows = jnp.where(same, own_rows, other_rows)
        in_units = jnp.where((exists & ~sends) | same, (in_rows + 15) >> 4, 0)
        out_total = out_total + out_units
        in_total = in_total + in_units
        mine[e] = out_units
        mine[8 + e] = own_block ^ (core * 16)
        mine[16 + e] = in_units
        mine[24 + e] = jnp.where(same, other_block, own_block) ^ (core * 16)
        mine[32 + e] = in_rows
    mine[40] = out_total
    mine[41] = in_total

    far = jnp.maximum(out_total - 2 * direct, 0)
    before = exact_dot(far, (x < y).astype(jnp.int32))
    total = jnp.sum(far, axis=1, keepdims=True)
    at_self = jnp.sum(jnp.where(same, before, 0), axis=1, keepdims=True)
    rank = before - at_self + jnp.where(y < x, total, 0)
    over_out = jnp.max((total + COLORS - 1) >> LOG_COLORS)
    over_in = jnp.zeros((), jnp.int32)
    earlier = (y < x).astype(jnp.int32)
    number, place, first = [], [], []
    for color in range(COLORS):
        first.append((color - rank) & (COLORS - 1))
        number.append((far - first[-1] + COLORS - 1) >> LOG_COLORS)
        over_in = jnp.maximum(over_in, jnp.max(jnp.sum(number[-1], axis=0, keepdims=True)))
        place.append(exact_dot(earlier, number[-1]))
    room = turns(direct)
    fits = (over_out <= items) & (over_in <= relayed) & (jnp.max(far) <= room * COLORS)
    fits_ref[0] = fits.astype(jnp.int32)
    odd = core == 1
    own_class = chip // (chips // CLASSES)
    hand_number = jnp.zeros(flat, jnp.int32)
    hand_place = jnp.zeros(flat, jnp.int32)
    hand_first = jnp.zeros(flat, jnp.int32)
    for k in range(CLASSES):
        picked = [jnp.where(odd, v[2 * k + 1], v[2 * k]) for v in (number, place, first)]
        for n, v in enumerate(picked):
            mine[47 + 6 * k + n] = flip(v)
        here = own_class == k
        hand_number = jnp.where(here, picked[0], hand_number)
        hand_place = jnp.where(here, picked[1], hand_place)
        hand_first = jnp.where(here, picked[2], hand_first)
    mine[42] = rank
    mine[43] = far
    own = pl.ds(chip, 1)

    out_units = [mine[e, own, :] for e in range(SHARE)]
    out_block = [mine[8 + e, own, :] for e in range(SHARE)]
    in_units = [mine[16 + e, own, :] for e in range(SHARE)]
    in_block = [mine[24 + e, own, :] for e in range(SHARE)]
    in_rows = [mine[32 + e, own, :] for e in range(SHARE)]
    out_total, in_total, rank_own, far_own = (mine[40 + k, own, :] for k in range(4))

    def lane(total):
        plain = jnp.minimum(total, 2 * direct)
        half = (plain + 1) >> 1
        return jnp.where(odd, half, 0), jnp.where(odd, plain - half, half)

    def unit_at(position, valid):
        value = jnp.full(position.shape, -1, jnp.int32)
        start = jnp.zeros((1, chips), jnp.int32)
        for e in range(SHARE):
            hit = valid & (position >= start) & (position < start + out_units[e])
            value = jnp.where(hit, out_block[e] * 8 + position - start, value)
            start = start + out_units[e]
        return value

    def code_at(position, valid):
        value = jnp.zeros(position.shape, jnp.int32)
        start = jnp.zeros((1, chips), jnp.int32)
        for e in range(SHARE):
            hit = valid & (position >= start) & (position < start + in_units[e])
            rows = jnp.minimum(in_rows[e] - UNIT * (position - start), UNIT)
            value = jnp.where(hit, in_block[e] * 32 + 32 + rows, value)
            start = start + in_units[e]
        return value

    step = lax.broadcasted_iota(jnp.int32, (direct, chips), 0)
    begin, length = lane(out_total)
    plain = unit_at(begin + step, step < length)
    send_ref[...] = jnp.maximum(plain, 0)
    target_ref[pl.ds(0, direct), :] = plain
    begin, length = lane(in_total)
    code_ref[...] = code_at(begin + step, step < length)

    if items:
        slot = lax.broadcasted_iota(jnp.int32, (items, chips), 0)
        place_in = lax.broadcasted_iota(jnp.int32, (relayed, chips), 0)
        for k in range(CLASSES):
            turn = COLORS * slot + 2 * k + core - rank_own
            unit = unit_at(2 * direct + turn, (turn >= 0) & (turn < far_own))
            far_ref[:, k : k + 1] = jnp.sum(jnp.maximum(unit, 0), axis=1, keepdims=True)
            number_t, place_t, first_t = (mine[47 + 6 * k + n, own, :] for n in range(3))
            made = jnp.zeros((relayed, chips), jnp.int32)
            for n in range(room):
                first = (2 * k + core - rank_own) & (COLORS - 1)
                target_ref[pl.ds(direct + CLASSES * n + k, 1), :] = unit_at(
                    2 * direct + first + COLORS * n, n < (far_own - first + COLORS - 1) >> LOG_COLORS
                )
                back_ref[pl.ds(CLASSES * n + k, 1), :] = jnp.where(n < number_t, place_t + n, -1)
                hit = (place_t + n == place_in) & (n < number_t)
                made = made + code_at(2 * direct + first_t + COLORS * n + 0 * place_in, hit)
            far_code_ref[:, k : k + 1] = jnp.sum(made, axis=1, keepdims=True)
        hand_number, hand_place, hand_from = (
            flip(hand_number), flip(hand_place), flip((rank + hand_first) >> LOG_COLORS)
        )
        for q in range(relayed):
            value = jnp.zeros(flat, jnp.int32)
            for n in range(room):
                hit = (hand_place + n == q) & (n < hand_number)
                value = value + jnp.where(hit, y * items + hand_from + n, 0)
            hand_ref[:, q : q + 1] = jnp.sum(value, axis=1, keepdims=True)


def make_plan(direct, items, relayed, told, device):
    devices, columns = told.shape
    chips = devices // 2
    ints = lambda *shape: jax.ShapeDtypeStruct(shape, jnp.int32)
    vmem = pl.BlockSpec(memory_space=pltpu.VMEM)
    return pl.pallas_call(
        functools.partial(plan_kernel, direct, items, relayed, chips),
        in_specs=[pl.BlockSpec(memory_space=pltpu.SMEM), vmem, vmem, vmem],
        out_specs=[vmem] * 7 + [pl.BlockSpec(memory_space=pltpu.SMEM)],
        out_shape=[
            ints(direct, chips),
            ints(max(items, 8), CLASSES),
            ints(direct, chips),
            ints(max(relayed, 8), CLASSES),
            ints(chips, max(relayed, 8)),
            ints(direct + turns(direct) * CLASSES, chips),
            ints(max(turns(direct), 1) * CLASSES, chips),
            ints(1),
        ],
        scratch_shapes=[
            pltpu.VMEM((SHARE, chips, chips), jnp.int32),
            pltpu.VMEM((SHARE, chips, chips), jnp.int32),
            pltpu.VMEM((4, 16, chips, devices), jnp.int32),
            pltpu.VMEM((44 + 6 * CLASSES, chips, chips), jnp.int32),
        ],
        compiler_params=pltpu.CompilerParams(vmem_limit_bytes=32 * MIB),
        cost_estimate=pl.CostEstimate(flops=10**11, bytes_accessed=10**6, transcendentals=0),
        name="plan",
    )(device.reshape(1), told[:, :devices], told[:, devices:], told[:, devices:].T)


def turn(first, second, values):
    rows = first * second
    o = lax.broadcasted_iota(jnp.int32, (rows, rows), 0)
    i = lax.broadcasted_iota(jnp.int32, (rows, rows), 1)
    take = ((o % first) * second + o // first == i).astype(jnp.float32).astype(jnp.bfloat16)
    return jnp.dot(take, values, preferred_element_type=jnp.float32).astype(jnp.bfloat16)


def fetch(near_ref, far_ref, held, sems):
    half = near_ref.shape[0]
    copies = [
        pltpu.make_async_copy(near_ref, held.at[pl.ds(0, half)], sems.at[0]),
        pltpu.make_async_copy(far_ref, held.at[pl.ds(half, half)], sems.at[1]),
    ]
    for copy in copies:
        copy.start()
    for copy in copies:
        copy.wait()


def pack_kernel(group, direct, items, send, far, near_ref, far_ref, out_ref, held, gathered, turned, sems):
    step = pl.program_id(0)
    chips = pl.num_programs(0) * group

    @pl.when(step == 0)
    def _():
        fetch(near_ref, far_ref, held, sems)
        if items:
            for p in range(CLASSES):
                for q in range(items):
                    gathered[pl.ds(q * UNIT, UNIT), :] = held[far[q * CLASSES + p]]
                size = items * UNIT
                turned[pl.ds(p * size, size), :] = turn(items, UNIT, gathered[...])

    for k in range(group):
        slot = step * group + k
        for p in range(direct):
            out_ref[k, pl.ds(p * UNIT, UNIT), :] = held[send[p * chips + slot]]
        if items:
            out_ref[k, pl.ds(direct * UNIT, items), :] = turned[pl.ds(pl.multiple_of(slot * items, items), items), :]


def pack(direct, items, send, far, near_units, far_units):
    units, _, depth = near_units.shape
    chips = send.shape[1]
    rows = direct * UNIT + items
    group = 4
    some = max(items, 16)
    return pl.pallas_call(
        functools.partial(pack_kernel, group, direct, items),
        grid_spec=pltpu.PrefetchScalarGridSpec(
            num_scalar_prefetch=2,
            grid=(chips // group,),
            in_specs=[pl.BlockSpec(memory_space=pl.ANY)] * 2,
            out_specs=pl.BlockSpec((group, rows, depth), lambda i, *_: (i, 0, 0)),
            scratch_shapes=[
                pltpu.VMEM((2 * units, UNIT, depth), jnp.bfloat16),
                pltpu.VMEM((some * UNIT, depth), jnp.bfloat16),
                pltpu.VMEM((some * chips, depth), jnp.bfloat16),
                pltpu.SemaphoreType.DMA((2,)),
            ],
        ),
        out_shape=jax.ShapeDtypeStruct((chips, rows, depth), jnp.bfloat16),
        compiler_params=pltpu.CompilerParams(vmem_limit_bytes=20 * MIB),
        name="pack",
    )(send.reshape(-1), far.reshape(-1), near_units, far_units)


def relay_kernel(hand_ref, held_ref, target_ref, back_ref, out_ref, target_out, back_out):
    target_out[...] = target_ref[...]
    back_out[...] = back_ref[...]
    held = held_ref[...]
    rows = held.shape[0] * held.shape[1]
    i = lax.broadcasted_iota(jnp.int32, (out_ref.shape[0], rows), 1)
    take = (hand_ref[...] == i).astype(jnp.float32).astype(jnp.bfloat16)
    out_ref[...] = jnp.dot(
        take, held.reshape(rows, held.shape[2]), preferred_element_type=jnp.float32
    ).astype(jnp.bfloat16)


def relay(hand, arrived, target, back, direct, items):
    chips, relayed = hand.shape
    depth = arrived.shape[2]
    step = chips * relayed // 2
    tables = [pl.BlockSpec(t.shape, lambda i: (0, 0)) for t in (target, back)]
    passed, target, back = pl.pallas_call(
        relay_kernel,
        grid=(chips * relayed // step,),
        in_specs=[
            pl.BlockSpec((step, 1), lambda i: (i, 0)),
            pl.BlockSpec((chips, items, depth), lambda i: (0, direct * UNIT // items, 0)),
            *tables,
        ],
        out_specs=[pl.BlockSpec((step, depth), lambda i: (i, 0)), *tables],
        out_shape=[
            jax.ShapeDtypeStruct((chips * relayed, depth), jnp.bfloat16),
            jax.ShapeDtypeStruct(target.shape, jnp.int32),
            jax.ShapeDtypeStruct(back.shape, jnp.int32),
        ],
        compiler_params=pltpu.CompilerParams(vmem_limit_bytes=54 * MIB),
        name="relay",
    )(hand.reshape(-1, 1), arrived, target, back)
    return passed.reshape(chips, relayed, depth), target, back


def score_kernel(
    places, group, turned, codes, counts, near, linked, near_ref, far_ref, arrived_ref, back_ref, best_ref,
    held, rows_held, batch, tiles, kept, head, follow, sems,
):
    slots = back_ref.shape[0]
    blocks, width, _ = held.shape
    copies = [
        pltpu.make_async_copy(near_ref, held.at[pl.ds(0, blocks // 2)], sems.at[0]),
        pltpu.make_async_copy(far_ref, held.at[pl.ds(blocks // 2, blocks // 2)], sems.at[1]),
    ]
    if turned:
        copies.insert(0, pltpu.make_async_copy(arrived_ref, rows_held, sems.at[2]))
    else:
        copies.append(pltpu.make_async_copy(arrived_ref.at[:, pl.ds(0, places * UNIT)], rows_held, sems.at[2]))
    for copy in copies:
        copy.start()
    best_ref[...] = jnp.full(best_ref.shape, -1.0, jnp.float32)
    tiles[...] = jnp.full(tiles.shape, -1.0, jnp.float32)

    def clear(b, carry):
        head[b] = -1
        return carry

    lax.fori_loop(0, blocks, clear, 0)

    def link(slot, carry):
        for p in range(places):
            made = codes[p * slots + slot]
            block = jnp.maximum((made >> 5) - 1, 0)
            unit = slot * 32 + p

            @pl.when(made > 0)
            def _():
                follow[unit] = head[block]
                head[block] = unit

        return carry

    lax.fori_loop(0, slots, link, 0)
    copies[0].wait()
    if turned:
        for slot in range(slots):
            rows_held[slot] = turn(UNIT, places, rows_held[slot])
    else:
        score_near(near, linked, counts, held, best_ref, kept)
    for copy in copies[1:]:
        copy.wait()

    i = lax.broadcasted_iota(jnp.int32, (UNIT, width), 0)
    j = lax.broadcasted_iota(jnp.int32, (UNIT, width), 1)

    def per_block(block, carry):
        columns = j < counts[block]

        def some_units(unit):
            taken = []
            for g in range(group):
                live = unit >= 0
                here = jnp.maximum(unit, 0)
                slot, p = here >> 5, here & 31
                batch[pl.ds(g * UNIT, UNIT), :] = rows_held[slot, pl.ds(pl.multiple_of(p * UNIT, UNIT), UNIT), :]
                rows = jnp.where(live, codes[p * slots + slot] & 31, 0)
                taken.append((jnp.where(live, slot, slots), p, rows))
                unit = jnp.where(live, follow[here], -1)
            scores = lax.dot_general(
                batch[...], held[block], (((1,), (1,)), ((), ())), preferred_element_type=jnp.float32
            )
            most = best_ref[pl.ds(block, 1), :]
            for g, (slot, p, rows) in enumerate(taken):
                tile = jnp.where((i < rows) & columns, scores[g * UNIT : (g + 1) * UNIT], -1.0)
                tiles[slot, pl.ds(pl.multiple_of(p * UNIT, UNIT), UNIT), :] = tile
                most = jnp.maximum(most, jnp.max(tile, axis=0, keepdims=True))
            best_ref[pl.ds(block, 1), :] = most
            return unit

        lax.while_loop(lambda unit: unit >= 0, some_units, head[block])
        return carry

    lax.fori_loop(0, blocks, per_block, 0)

    if slots % 8 == 0:

        def finish(part, carry):
            for k in range(8):
                slot = part * 8 + k
                back_ref[pl.ds(slot, 1), :] = jnp.max(tiles[slot].T, axis=0, keepdims=True)
            return carry

        lax.fori_loop(0, slots // 8, finish, 0)
    else:
        for slot in range(slots):
            back_ref[slot : slot + 1, :] = jnp.max(tiles[slot].T, axis=0, keepdims=True)


def score(codes, counts, linked, near, far, arrived, group, turned):
    blocks, width, depth = near.shape
    places, slots = codes.shape
    rows = places * UNIT
    any_place = pl.BlockSpec(memory_space=pl.ANY)
    vmem = pl.BlockSpec(memory_space=pltpu.VMEM)
    smem = pl.BlockSpec(memory_space=pltpu.SMEM)
    return pl.pallas_call(
        functools.partial(score_kernel, places, group, turned),
        in_specs=[smem, smem, smem, smem, any_place, any_place, any_place],
        out_specs=[vmem, vmem],
        out_shape=[
            jax.ShapeDtypeStruct((slots, rows), jnp.float32),
            jax.ShapeDtypeStruct((2 * blocks, width), jnp.float32),
        ],
        scratch_shapes=[
            pltpu.VMEM((2 * blocks, width, depth), jnp.bfloat16),
            pltpu.VMEM((slots, rows, depth), jnp.bfloat16),
            pltpu.VMEM((group * UNIT, depth), jnp.bfloat16),
            pltpu.VMEM((slots + 1, rows, width), jnp.float32),
            pltpu.VMEM((8 if turned else blocks, width, width), jnp.float32),
            pltpu.SMEM((2 * blocks,), jnp.int32),
            pltpu.SMEM((slots * 32,), jnp.int32),
            pltpu.SemaphoreType.DMA((3,)),
        ],
        compiler_params=pltpu.CompilerParams(vmem_limit_bytes=(24 if turned else 56) * MIB),
        cost_estimate=pl.CostEstimate(
            flops=2 * slots * rows * width * depth, bytes_accessed=2 * slots * rows * depth, transcendentals=0
        ),
        name="score",
    )(codes.reshape(-1), counts, jnp.asarray(near_pairs(blocks).reshape(-1)), linked, near, far, arrived)


def one_hot(index, count, valid):
    return (index[:, None] == jnp.arange(count, dtype=jnp.int32)[None, :]) & valid[:, None]


def exchange(values, chips):
    groups = [[2 * x + c for x in range(chips)] for c in range(2)]
    return lax.all_to_all(values, "shard", split_axis=0, concat_axis=0, axis_index_groups=groups, tiled=True)


def far_maxima(direct, items, relayed, plan, counts, linked, near, far):
    send, own_far, codes, far_codes, hand, target, item_back, _ = plan
    blocks, width, depth = near.shape
    chips = send.shape[1]
    outgoing = pack(
        direct, items, send, own_far,
        near.reshape(-1, UNIT, depth), far.reshape(-1, UNIT, depth),
    )
    arrived = exchange(outgoing, chips)
    arrived, near, far, counts, linked, codes, far_codes, hand, target, item_back = lax.optimization_barrier(
        (arrived, near, far, counts, linked, codes, far_codes, hand, target, item_back)
    )
    if items:
        passed, target, item_back = relay(hand, arrived, target, item_back, direct, items)
        gained = exchange(passed, chips)
    back, best = score(codes, counts, linked, near, far, arrived, 16, False)
    places = direct
    if items:
        gained = gained.reshape(CLASSES, chips // CLASSES * relayed, depth)
        far_back, far_best = score(far_codes, counts, linked, near, far, gained, 4, True)
        best = jnp.maximum(best, far_best)
        hit = item_back.reshape(turns(direct), CLASSES, chips)[..., None] == jnp.arange(relayed, dtype=jnp.int32)
        far_back = far_back.reshape(1, CLASSES, 1, relayed, UNIT)
        far_back = jnp.where(hit[..., None], far_back, -1.0).max(axis=3)
        far_back = far_back.transpose(2, 0, 1, 3).reshape(chips, -1)
        back = jnp.concatenate([back, far_back], axis=1)
        places = direct + turns(direct) * CLASSES
    returned = exchange(back, chips)
    spots = target.T.reshape(-1)
    values = returned.reshape(-1, UNIT).T
    hit = spots[:, None] == jnp.arange(2 * blocks * width // UNIT, dtype=jnp.int32)[None, :]
    folded = jnp.where(hit[None], values[:, :, None], -1.0).max(axis=1)
    best = jnp.maximum(best, folded.T.reshape(2 * blocks, width))
    other = lax.ppermute(best[blocks:], "shard", [(d, d ^ 1) for d in range(2 * chips)])
    return jnp.maximum(best[:blocks], other)


def on_device(embeddings, block_rows, pairs):
    blocks = block_rows.shape[0]
    width = embeddings.shape[0] // blocks
    peers = lax.axis_size("shard")
    myself = lax.axis_index("shard")
    swap = [(d, d ^ 1) for d in range(peers)]
    row_block, col_block = pairs[:, 0], pairs[:, 1]
    alive = pairs[:, 2] == myself
    owner = row_block // blocks
    remote = alive & (owner != myself)
    row_local, col_local = row_block % blocks, col_block % blocks
    tell = ask(myself, pairs, block_rows, peers)
    told = lax.all_to_all(tell, "shard", split_axis=0, concat_axis=0, tiled=True)[:, 0]

    unit = normalize(embeddings, tell)
    near = unit.reshape(blocks, width, -1)
    far = lax.ppermute(near, "shard", swap)

    nearby = alive & ~remote
    row_table = one_hot(row_local, blocks, nearby).astype(jnp.float32)
    col_table = one_hot(col_local, blocks, nearby).astype(jnp.float32)
    adjacency = (
        lax.dot_general(row_table, col_table, (((0,), (0,)), ((), ())), preferred_element_type=jnp.float32) > 0.5
    )
    linked = (adjacency | adjacency.T).astype(jnp.int32).reshape(-1)

    plan = make_plan(*PLANS[0], told, myself)
    counts = jnp.concatenate([block_rows, lax.dynamic_slice_in_dim(told, myself ^ 1, 1, 0)[0, peers:]])

    def attempt(level, plan):
        def here():
            return far_maxima(*PLANS[level], plan, counts, linked, near, far)

        def later():
            return attempt(level + 1, make_plan(*PLANS[level + 1], told, myself))

        return lax.cond(plan[-1][0] > 0, here, later) if level + 1 < len(PLANS) else here()

    return attempt(0, plan)


def solution(mesh):
    placed = (P("shard", None), P("shard"), P("shard", None))
    return jax.shard_map(
        on_device, mesh=mesh, in_specs=placed, out_specs=P("shard", None), check_vma=False
    )
```

```python
import functools

import jax
import jax.numpy as jnp
import numpy as np
from jax import lax
from jax.experimental import pallas as pl
from jax.experimental.pallas import tpu as pltpu
from jax.sharding import PartitionSpec as P

UNIT = 16
CLASSES = 4
COLORS = 2 * CLASSES
LOG_COLORS = 3
PLANS = ((7, 16, 24), (8, 16, 16), (16, 0, 0))
SHARE = 8
MIB = 1024 * 1024


def turns(direct):
    return -(-(2 * 16 - 2 * direct) // COLORS)


def ask_kernel(me_ref, pairs_ref, rows_ref, tell_ref):
    device = me_ref[0]
    peers, _, columns = tell_ref.shape
    row, col = pairs_ref[0:1, :], pairs_ref[1:2, :]
    owner = row >> 4
    far = (pairs_ref[2:3, :] == device) & (owner != device)
    peer = lax.broadcasted_iota(jnp.int32, (peers, row.shape[1]), 0)
    code = (row & 15) * 16 + (col & 15)
    code = jnp.where((owner == peer) & far, code, -1).astype(jnp.float32)
    most = code[:, :peers]
    for k in range(1, row.shape[1] // peers):
        most = jnp.maximum(most, code[:, k * peers : (k + 1) * peers])
    wanted = jnp.max(most.T, axis=0, keepdims=True).astype(jnp.int32)
    tell = jnp.concatenate([wanted, rows_ref[...]], axis=1)
    tell_ref[...] = jnp.broadcast_to(tell[None], tell_ref.shape)


def ask(device, pairs, block_rows, peers):
    blocks = block_rows.shape[0]
    assert blocks == 16
    vmem = pl.BlockSpec(memory_space=pltpu.VMEM)
    return pl.pallas_call(
        ask_kernel,
        in_specs=[pl.BlockSpec(memory_space=pltpu.SMEM), vmem, vmem],
        out_specs=vmem,
        out_shape=jax.ShapeDtypeStruct((peers, 1, peers + blocks), jnp.int32),
        name="ask",
    )(device.reshape(1), pairs.T, block_rows.reshape(1, blocks))


def normalize_kernel(after_ref, values_ref, unit_ref):
    values = values_ref[...].astype(jnp.float32)
    total = jnp.sum(values * values, axis=-1, keepdims=True)
    unit_ref[...] = (values * lax.rsqrt(total + 1e-06)).astype(jnp.bfloat16)


def normalize(embeddings, after):
    rows, depth = embeddings.shape
    step = 1024
    return pl.pallas_call(
        normalize_kernel,
        grid=(rows // step,),
        in_specs=[pl.BlockSpec(memory_space=pl.ANY), pl.BlockSpec((step, depth), lambda i: (i, 0))],
        out_specs=pl.BlockSpec((step, depth), lambda i: (i, 0)),
        out_shape=jax.ShapeDtypeStruct((rows, depth), jnp.bfloat16),
        cost_estimate=pl.CostEstimate(flops=4 * rows * depth, bytes_accessed=4 * rows * depth, transcendentals=rows),
        name="normalize",
    )(after, embeddings)


def near_pairs(blocks):
    return np.array([(i, j) for i in range(blocks // 4) for j in range(blocks // 2) if (j + 1) * 2 > i * 4], np.int32)


def score_near(near, linked, counts, rows_ref, best_ref, kept):
    blocks, width, depth = rows_ref.shape[0] // 2, rows_ref.shape[1], rows_ref.shape[2]
    kept[...] = jnp.full(kept.shape, -1.0, jnp.float32)
    i = lax.broadcasted_iota(jnp.int32, (width, width), 0)
    j = lax.broadcasted_iota(jnp.int32, (width, width), 1)

    def step(number, carry):
        left, right = near[2 * number], near[2 * number + 1]
        rows = rows_ref[pl.ds(left * 4, 4)].reshape(4 * width, depth)
        cols = rows_ref[pl.ds(right * 2, 2)].reshape(2 * width, depth)
        scores = lax.dot_general(rows, cols, (((1,), (1,)), ((), ())), preferred_element_type=jnp.float32)
        for b in range(2):
            c = right * 2 + b
            most = best_ref[pl.ds(c, 1), :]
            for a in range(4):
                r = left * 4 + a
                limit = jnp.where(linked[r * blocks + c] > 0, counts[r], 0)
                keep = (i < limit) & (j < counts[c]) & ((r != c) | (i != j))
                part = jnp.where(keep, scores[a * width : (a + 1) * width, b * width : (b + 1) * width], -1.0)
                kept[r] = jnp.maximum(kept[r], part)
                most = jnp.maximum(most, jnp.max(part, axis=0, keepdims=True))
            best_ref[pl.ds(c, 1), :] = most
        return carry

    lax.fori_loop(0, len(near_pairs(blocks)), step, 0)
    for b in range(blocks):
        best_ref[pl.ds(b, 1), :] = jnp.maximum(best_ref[pl.ds(b, 1), :], jnp.max(kept[b].T, axis=0, keepdims=True))


def exact_dot(a, b):
    return jnp.dot(
        a.astype(jnp.float32).astype(jnp.bfloat16),
        b.astype(jnp.float32).astype(jnp.bfloat16),
        preferred_element_type=jnp.float32,
    ).astype(jnp.int32)


def flip(a):
    return a.astype(jnp.float32).T.astype(jnp.int32)


def plan_kernel(
    direct, items, relayed, chips, me_ref, pair_ref, count_ref, count_t_ref,
    send_ref, far_ref, code_ref, far_code_ref, hand_ref, target_ref, back_ref, fits_ref,
    w_lo, w_hi, sums, mine,
):
    device = me_ref[0]
    chip, core = device // 2, device % 2
    devices = 2 * chips
    flat = (chips, chips)
    pair = pair_ref[...]
    code = jnp.maximum(pair, 0)
    row_of, col_of = code >> 4, code & 15
    row_count = jnp.zeros(pair.shape, jnp.int32)
    col_count = jnp.zeros(pair.shape, jnp.int32)
    for l in range(16):
        row_count = jnp.where(row_of == l, count_t_ref[pl.ds(l, 1), :], row_count)
        col_count = jnp.where(col_of == l, count_ref[:, l : l + 1], col_count)

    xs = lax.broadcasted_iota(jnp.int32, (chips, devices), 0)
    ds = lax.broadcasted_iota(jnp.int32, (chips, devices), 1)
    pick = [(ds == 2 * xs + i).astype(jnp.int32) for i in range(2)]
    pick_t = [flip(p) for p in pick]

    def split(values):
        half = [exact_dot(p, values) for p in pick]
        return [[exact_dot(half[i], pick_t[j]) for j in range(2)] for i in range(2)]

    asked = {"code": split(pair + 1), "row": split(row_count), "col": split(col_count)}
    asked_t = {k: [[flip(v[j][i]) for j in range(2)] for i in range(2)] for k, v in asked.items()}

    x = lax.broadcasted_iota(jnp.int32, flat, 0)
    y = lax.broadcasted_iota(jnp.int32, flat, 1)
    low, same = x <= y, x == y
    edges = []
    for kind in range(2):
        for p in range(2):
            for q in range(2):
                first, second = (asked_t, asked) if kind == 0 else (asked, asked_t)
                here = {k: jnp.where(low, first[k][p][q], second[k][q][p]) for k in asked}
                exists = here["code"] > 0
                if kind == 1:
                    exists = exists & ~same
                number = jnp.maximum(here["code"] - 1, 0)
                r, c = number >> 4, number & 15
                side = jnp.where(low, p, q) * 16
                other = jnp.where(low, q, p) * 16
                owns_row = low if kind == 0 else ~low
                own_block = side + jnp.where(owns_row, r, c)
                other_block = other + jnp.where(owns_row, c, r)
                own_rows = jnp.where(exists, jnp.where(owns_row, here["row"], here["col"]), 0)
                other_rows = jnp.where(exists, jnp.where(owns_row, here["col"], here["row"]), 0)
                edges.append((exists, own_block, other_block, own_rows, other_rows))
    for e, (exists, _, _, own_rows, other_rows) in enumerate(edges):
        own_units, other_units = (own_rows + 15) >> 4, (other_rows + 15) >> 4
        w_lo[e] = jnp.where(low, own_units, other_units)
        w_hi[e] = jnp.where(low, other_units, own_units)

    for half in range(2):
        for choice in range(16):
            up = jnp.zeros(flat, jnp.int32)
            down = jnp.zeros(flat, jnp.int32)
            for b in range(4):
                if choice >> b & 1:
                    up = up + w_lo[half * 4 + b]
                else:
                    down = down + w_hi[half * 4 + b]
            lanes = pl.ds(0, chips) if half or choice < 8 else pl.ds(chips, chips)
            spot = choice if half else choice % 8
            sums[half, spot, :, lanes] = up
            sums[2 + half, spot, :, lanes] = down
            if half:
                sums[1, spot, :, pl.ds(chips, chips)] = up
                sums[3, spot, :, pl.ds(chips, chips)] = down
    eight = jnp.where(lax.broadcasted_iota(jnp.int32, (chips, devices), 1) < chips, 0, 8)

    def try_half(a, least):
        up_a, down_a = sums[0, a] - 2 * direct, sums[2, a] - 2 * direct
        for b in range(16):
            up, down = up_a + sums[1, b], down_a + sums[3, b]
            over = jnp.maximum(up, 0) + jnp.maximum(down, 0)
            rank = over * 65536 + jnp.maximum(up, down) * 256 + (b * 16 + a) + eight
            least = jnp.minimum(least, rank)
        return least

    least = lax.fori_loop(0, 8, try_half, jnp.full((chips, devices), 2**30, jnp.int32))
    least = jnp.minimum(least[:, :chips], least[:, chips:])
    chosen = jnp.where(same, 255, least & 255)

    out_total = jnp.zeros(flat, jnp.int32)
    in_total = jnp.zeros(flat, jnp.int32)
    for e, (exists, own_block, other_block, own_rows, other_rows) in enumerate(edges):
        bit = (chosen >> e) & 1
        sends = exists & ((bit == 1) == low)
        out_units = jnp.where(sends, (own_rows + 15) >> 4, 0)
        in_rows = jnp.where(same, own_rows, other_rows)
        in_units = jnp.where((exists & ~sends) | same, (in_rows + 15) >> 4, 0)
        out_total = out_total + out_units
        in_total = in_total + in_units
        mine[e] = out_units
        mine[8 + e] = own_block ^ (core * 16)
        mine[16 + e] = in_units
        mine[24 + e] = jnp.where(same, other_block, own_block) ^ (core * 16)
        mine[32 + e] = in_rows
    mine[40] = out_total
    mine[41] = in_total

    far = jnp.maximum(out_total - 2 * direct, 0)
    before = exact_dot(far, (x < y).astype(jnp.int32))
    total = jnp.sum(far, axis=1, keepdims=True)
    at_self = jnp.sum(jnp.where(same, before, 0), axis=1, keepdims=True)
    rank = before - at_self + jnp.where(y < x, total, 0)
    over_out = jnp.max((total + COLORS - 1) >> LOG_COLORS)
    over_in = jnp.zeros((), jnp.int32)
    earlier = (y < x).astype(jnp.int32)
    number, place, first = [], [], []
    for color in range(COLORS):
        first.append((color - rank) & (COLORS - 1))
        number.append((far - first[-1] + COLORS - 1) >> LOG_COLORS)
        over_in = jnp.maximum(over_in, jnp.max(jnp.sum(number[-1], axis=0, keepdims=True)))
        place.append(exact_dot(earlier, number[-1]))
    room = turns(direct)
    fits = (over_out <= items) & (over_in <= relayed) & (jnp.max(far) <= room * COLORS)
    fits_ref[0] = fits.astype(jnp.int32)
    odd = core == 1
    own_class = chip // (chips // CLASSES)
    hand_number = jnp.zeros(flat, jnp.int32)
    hand_place = jnp.zeros(flat, jnp.int32)
    hand_first = jnp.zeros(flat, jnp.int32)
    for k in range(CLASSES):
        picked = [jnp.where(odd, v[2 * k + 1], v[2 * k]) for v in (number, place, first)]
        for n, v in enumerate(picked):
            mine[47 + 6 * k + n] = flip(v)
        here = own_class == k
        hand_number = jnp.where(here, picked[0], hand_number)
        hand_place = jnp.where(here, picked[1], hand_place)
        hand_first = jnp.where(here, picked[2], hand_first)
    mine[42] = rank
    mine[43] = far
    own = pl.ds(chip, 1)

    out_units = [mine[e, own, :] for e in range(SHARE)]
    out_block = [mine[8 + e, own, :] for e in range(SHARE)]
    in_units = [mine[16 + e, own, :] for e in range(SHARE)]
    in_block = [mine[24 + e, own, :] for e in range(SHARE)]
    in_rows = [mine[32 + e, own, :] for e in range(SHARE)]
    out_total, in_total, rank_own, far_own = (mine[40 + k, own, :] for k in range(4))

    def lane(total):
        plain = jnp.minimum(total, 2 * direct)
        half = (plain + 1) >> 1
        return jnp.where(odd, half, 0), jnp.where(odd, plain - half, half)

    def unit_at(position, valid):
        value = jnp.full(position.shape, -1, jnp.int32)
        start = jnp.zeros((1, chips), jnp.int32)
        for e in range(SHARE):
            hit = valid & (position >= start) & (position < start + out_units[e])
            value = jnp.where(hit, out_block[e] * 8 + position - start, value)
            start = start + out_units[e]
        return value

    def code_at(position, valid):
        value = jnp.zeros(position.shape, jnp.int32)
        start = jnp.zeros((1, chips), jnp.int32)
        for e in range(SHARE):
            hit = valid & (position >= start) & (position < start + in_units[e])
            rows = jnp.minimum(in_rows[e] - UNIT * (position - start), UNIT)
            value = jnp.where(hit, in_block[e] * 32 + 32 + rows, value)
            start = start + in_units[e]
        return value

    step = lax.broadcasted_iota(jnp.int32, (direct, chips), 0)
    begin, length = lane(out_total)
    plain = unit_at(begin + step, step < length)
    send_ref[...] = jnp.maximum(plain, 0)
    target_ref[pl.ds(0, direct), :] = plain
    begin, length = lane(in_total)
    code_ref[...] = code_at(begin + step, step < length)

    if items:
        slot = lax.broadcasted_iota(jnp.int32, (items, chips), 0)
        place_in = lax.broadcasted_iota(jnp.int32, (relayed, chips), 0)
        for k in range(CLASSES):
            turn = COLORS * slot + 2 * k + core - rank_own
            unit = unit_at(2 * direct + turn, (turn >= 0) & (turn < far_own))
            far_ref[:, k : k + 1] = jnp.sum(jnp.maximum(unit, 0), axis=1, keepdims=True)
            number_t, place_t, first_t = (mine[47 + 6 * k + n, own, :] for n in range(3))
            made = jnp.zeros((relayed, chips), jnp.int32)
            for n in range(room):
                first = (2 * k + core - rank_own) & (COLORS - 1)
                target_ref[pl.ds(direct + CLASSES * n + k, 1), :] = unit_at(
                    2 * direct + first + COLORS * n, n < (far_own - first + COLORS - 1) >> LOG_COLORS
                )
                back_ref[pl.ds(CLASSES * n + k, 1), :] = jnp.where(n < number_t, place_t + n, -1)
                hit = (place_t + n == place_in) & (n < number_t)
                made = made + code_at(2 * direct + first_t + COLORS * n + 0 * place_in, hit)
            far_code_ref[:, k : k + 1] = jnp.sum(made, axis=1, keepdims=True)
        hand_number, hand_place, hand_from = (
            flip(hand_number), flip(hand_place), flip((rank + hand_first) >> LOG_COLORS)
        )
        for q in range(relayed):
            value = jnp.zeros(flat, jnp.int32)
            for n in range(room):
                hit = (hand_place + n == q) & (n < hand_number)
                value = value + jnp.where(hit, y * items + hand_from + n, 0)
            hand_ref[:, q : q + 1] = jnp.sum(value, axis=1, keepdims=True)


def make_plan(direct, items, relayed, told, device):
    devices, columns = told.shape
    chips = devices // 2
    ints = lambda *shape: jax.ShapeDtypeStruct(shape, jnp.int32)
    vmem = pl.BlockSpec(memory_space=pltpu.VMEM)
    return pl.pallas_call(
        functools.partial(plan_kernel, direct, items, relayed, chips),
        in_specs=[pl.BlockSpec(memory_space=pltpu.SMEM), vmem, vmem, vmem],
        out_specs=[vmem] * 7 + [pl.BlockSpec(memory_space=pltpu.SMEM)],
        out_shape=[
            ints(direct, chips),
            ints(max(items, 8), CLASSES),
            ints(direct, chips),
            ints(max(relayed, 8), CLASSES),
            ints(chips, max(relayed, 8)),
            ints(direct + turns(direct) * CLASSES, chips),
            ints(max(turns(direct), 1) * CLASSES, chips),
            ints(1),
        ],
        scratch_shapes=[
            pltpu.VMEM((SHARE, chips, chips), jnp.int32),
            pltpu.VMEM((SHARE, chips, chips), jnp.int32),
            pltpu.VMEM((4, 16, chips, devices), jnp.int32),
            pltpu.VMEM((44 + 6 * CLASSES, chips, chips), jnp.int32),
        ],
        compiler_params=pltpu.CompilerParams(vmem_limit_bytes=32 * MIB),
        cost_estimate=pl.CostEstimate(flops=10**11, bytes_accessed=10**6, transcendentals=0),
        name="plan",
    )(device.reshape(1), told[:, :devices], told[:, devices:], told[:, devices:].T)


def turn(first, second, values):
    rows = first * second
    o = lax.broadcasted_iota(jnp.int32, (rows, rows), 0)
    i = lax.broadcasted_iota(jnp.int32, (rows, rows), 1)
    take = ((o % first) * second + o // first == i).astype(jnp.float32).astype(jnp.bfloat16)
    return jnp.dot(take, values, preferred_element_type=jnp.float32).astype(jnp.bfloat16)


def fetch(near_ref, far_ref, held, sems):
    half = near_ref.shape[0]
    copies = [
        pltpu.make_async_copy(near_ref, held.at[pl.ds(0, half)], sems.at[0]),
        pltpu.make_async_copy(far_ref, held.at[pl.ds(half, half)], sems.at[1]),
    ]
    for copy in copies:
        copy.start()
    for copy in copies:
        copy.wait()


def pack_kernel(group, direct, items, send, far, near_ref, far_ref, out_ref, held, gathered, turned, sems):
    step = pl.program_id(0)
    chips = pl.num_programs(0) * group

    @pl.when(step == 0)
    def _():
        fetch(near_ref, far_ref, held, sems)
        if items:
            for p in range(CLASSES):
                for q in range(items):
                    gathered[pl.ds(q * UNIT, UNIT), :] = held[far[q * CLASSES + p]]
                size = items * UNIT
                turned[pl.ds(p * size, size), :] = turn(items, UNIT, gathered[...])

    for k in range(group):
        slot = step * group + k
        for p in range(direct):
            out_ref[k, pl.ds(p * UNIT, UNIT), :] = held[send[p * chips + slot]]
        if items:
            out_ref[k, pl.ds(direct * UNIT, items), :] = turned[pl.ds(pl.multiple_of(slot * items, items), items), :]


def pack(direct, items, send, far, near_units, far_units):
    units, _, depth = near_units.shape
    chips = send.shape[1]
    rows = direct * UNIT + items
    group = 8 if items else 4
    some = max(items, 16)
    return pl.pallas_call(
        functools.partial(pack_kernel, group, direct, items),
        grid_spec=pltpu.PrefetchScalarGridSpec(
            num_scalar_prefetch=2,
            grid=(chips // group,),
            in_specs=[pl.BlockSpec(memory_space=pl.ANY)] * 2,
            out_specs=pl.BlockSpec((group, rows, depth), lambda i, *_: (i, 0, 0)),
            scratch_shapes=[
                pltpu.VMEM((2 * units, UNIT, depth), jnp.bfloat16),
                pltpu.VMEM((some * UNIT, depth), jnp.bfloat16),
                pltpu.VMEM((some * chips, depth), jnp.bfloat16),
                pltpu.SemaphoreType.DMA((2,)),
            ],
        ),
        out_shape=jax.ShapeDtypeStruct((chips, rows, depth), jnp.bfloat16),
        compiler_params=pltpu.CompilerParams(vmem_limit_bytes=20 * MIB),
        name="pack",
    )(send.reshape(-1), far.reshape(-1), near_units, far_units)


def relay_kernel(hand_ref, held_ref, target_ref, back_ref, out_ref, target_out, back_out):
    target_out[...] = target_ref[...]
    back_out[...] = back_ref[...]
    held = held_ref[...]
    rows = held.shape[0] * held.shape[1]
    hand = hand_ref[...]
    slots, relayed = hand.shape
    o = lax.broadcasted_iota(jnp.int32, (slots * relayed, slots), 0)
    spread = (o // relayed == lax.broadcasted_iota(jnp.int32, o.shape, 1)).astype(jnp.int32)
    each = exact_dot(spread, hand >> 4) * 16 + exact_dot(spread, hand & 15)
    o = lax.broadcasted_iota(jnp.int32, each.shape, 0)
    own = o % relayed == lax.broadcasted_iota(jnp.int32, each.shape, 1)
    source = jnp.sum(jnp.where(own, each, 0), axis=1, keepdims=True)
    i = lax.broadcasted_iota(jnp.int32, (out_ref.shape[0], rows), 1)
    take = (source == i).astype(jnp.float32).astype(jnp.bfloat16)
    out_ref[...] = jnp.dot(
        take, held.reshape(rows, held.shape[2]), preferred_element_type=jnp.float32
    ).astype(jnp.bfloat16)


def relay(hand, arrived, target, back, direct, items):
    chips, relayed = hand.shape
    depth = arrived.shape[2]
    step = chips * relayed // 2
    tables = [pl.BlockSpec(t.shape, lambda i: (0, 0)) for t in (target, back)]
    passed, target, back = pl.pallas_call(
        relay_kernel,
        grid=(chips * relayed // step,),
        in_specs=[
            pl.BlockSpec((chips // 2, relayed), lambda i: (i, 0)),
            pl.BlockSpec((chips, items, depth), lambda i: (0, direct * UNIT // items, 0)),
            *tables,
        ],
        out_specs=[pl.BlockSpec((step, depth), lambda i: (i, 0)), *tables],
        out_shape=[
            jax.ShapeDtypeStruct((chips * relayed, depth), jnp.bfloat16),
            jax.ShapeDtypeStruct(target.shape, jnp.int32),
            jax.ShapeDtypeStruct(back.shape, jnp.int32),
        ],
        compiler_params=pltpu.CompilerParams(vmem_limit_bytes=54 * MIB),
        name="relay",
    )(hand, arrived, target, back)
    return passed.reshape(chips, relayed, depth), target, back


def score_kernel(
    places, group, turned, codes, counts, near, linked, near_ref, far_ref, arrived_ref, back_ref, best_ref,
    held, rows_held, batch, tiles, kept, head, follow, sems,
):
    slots = back_ref.shape[0]
    blocks, width, _ = held.shape
    copies = [
        pltpu.make_async_copy(near_ref, held.at[pl.ds(0, blocks // 2)], sems.at[0]),
        pltpu.make_async_copy(far_ref, held.at[pl.ds(blocks // 2, blocks // 2)], sems.at[1]),
    ]
    if turned:
        copies.insert(0, pltpu.make_async_copy(arrived_ref, rows_held, sems.at[2]))
    else:
        copies.append(pltpu.make_async_copy(arrived_ref.at[:, pl.ds(0, places * UNIT)], rows_held, sems.at[2]))
    for copy in copies:
        copy.start()
    best_ref[...] = jnp.full(best_ref.shape, -1.0, jnp.float32)
    tiles[...] = jnp.full(tiles.shape, -1.0, jnp.float32)

    def clear(b, carry):
        head[b] = -1
        return carry

    lax.fori_loop(0, blocks, clear, 0)

    def link(slot, carry):
        for p in range(places):
            made = codes[p * slots + slot]
            block = jnp.maximum((made >> 5) - 1, 0)
            unit = slot * 32 + p

            @pl.when(made > 0)
            def _():
                follow[unit] = head[block]
                head[block] = unit

        return carry

    lax.fori_loop(0, slots, link, 0)
    copies[0].wait()
    if turned:
        for slot in range(slots):
            rows_held[slot] = turn(UNIT, places, rows_held[slot])
    else:
        score_near(near, linked, counts, held, best_ref, kept)
    for copy in copies[1:]:
        copy.wait()

    i = lax.broadcasted_iota(jnp.int32, (UNIT, width), 0)
    j = lax.broadcasted_iota(jnp.int32, (UNIT, width), 1)

    def per_block(block, carry):
        columns = j < counts[block]

        def some_units(unit):
            taken = []
            for g in range(group):
                live = unit >= 0
                here = jnp.maximum(unit, 0)
                slot, p = here >> 5, here & 31
                batch[pl.ds(g * UNIT, UNIT), :] = rows_held[slot, pl.ds(pl.multiple_of(p * UNIT, UNIT), UNIT), :]
                rows = jnp.where(live, codes[p * slots + slot] & 31, 0)
                taken.append((jnp.where(live, slot, slots), p, rows))
                unit = jnp.where(live, follow[here], -1)
            scores = lax.dot_general(
                batch[...], held[block], (((1,), (1,)), ((), ())), preferred_element_type=jnp.float32
            )
            most = best_ref[pl.ds(block, 1), :]
            for g, (slot, p, rows) in enumerate(taken):
                tile = jnp.where((i < rows) & columns, scores[g * UNIT : (g + 1) * UNIT], -1.0)
                tiles[slot, pl.ds(pl.multiple_of(p * UNIT, UNIT), UNIT), :] = tile
                most = jnp.maximum(most, jnp.max(tile, axis=0, keepdims=True))
            best_ref[pl.ds(block, 1), :] = most
            return unit

        lax.while_loop(lambda unit: unit >= 0, some_units, head[block])
        return carry

    lax.fori_loop(0, blocks, per_block, 0)

    if slots % 8 == 0:

        def finish(part, carry):
            for k in range(8):
                slot = part * 8 + k
                back_ref[pl.ds(slot, 1), :] = jnp.max(tiles[slot].T, axis=0, keepdims=True)
            return carry

        lax.fori_loop(0, slots // 8, finish, 0)
    else:
        for slot in range(slots):
            back_ref[slot : slot + 1, :] = jnp.max(tiles[slot].T, axis=0, keepdims=True)


def score(codes, counts, linked, near, far, arrived, group, turned):
    blocks, width, depth = near.shape
    places, slots = codes.shape
    rows = places * UNIT
    any_place = pl.BlockSpec(memory_space=pl.ANY)
    vmem = pl.BlockSpec(memory_space=pltpu.VMEM)
    smem = pl.BlockSpec(memory_space=pltpu.SMEM)
    return pl.pallas_call(
        functools.partial(score_kernel, places, group, turned),
        in_specs=[smem, smem, smem, smem, any_place, any_place, any_place],
        out_specs=[vmem, vmem],
        out_shape=[
            jax.ShapeDtypeStruct((slots, rows), jnp.float32),
            jax.ShapeDtypeStruct((2 * blocks, width), jnp.float32),
        ],
        scratch_shapes=[
            pltpu.VMEM((2 * blocks, width, depth), jnp.bfloat16),
            pltpu.VMEM((slots, rows, depth), jnp.bfloat16),
            pltpu.VMEM((group * UNIT, depth), jnp.bfloat16),
            pltpu.VMEM((slots + 1, rows, width), jnp.float32),
            pltpu.VMEM((8 if turned else blocks, width, width), jnp.float32),
            pltpu.SMEM((2 * blocks,), jnp.int32),
            pltpu.SMEM((slots * 32,), jnp.int32),
            pltpu.SemaphoreType.DMA((3,)),
        ],
        compiler_params=pltpu.CompilerParams(vmem_limit_bytes=(24 if turned else 45 if places <= 8 else 56) * MIB),
        cost_estimate=pl.CostEstimate(
            flops=2 * slots * rows * width * depth, bytes_accessed=2 * slots * rows * depth, transcendentals=0
        ),
        name="score",
    )(codes.reshape(-1), counts, jnp.asarray(near_pairs(blocks).reshape(-1)), linked, near, far, arrived)


def one_hot(index, count, valid):
    return (index[:, None] == jnp.arange(count, dtype=jnp.int32)[None, :]) & valid[:, None]


def exchange(values, chips):
    groups = [[2 * x + c for x in range(chips)] for c in range(2)]
    return lax.all_to_all(values, "shard", split_axis=0, concat_axis=0, axis_index_groups=groups, tiled=True)


def far_maxima(direct, items, relayed, plan, counts, linked, near, far):
    send, own_far, codes, far_codes, hand, target, item_back, _ = plan
    blocks, width, depth = near.shape
    chips = send.shape[1]
    outgoing = pack(
        direct, items, send, own_far,
        near.reshape(-1, UNIT, depth), far.reshape(-1, UNIT, depth),
    )
    arrived = exchange(outgoing, chips)
    arrived, near, far, counts, linked, codes, far_codes, hand, target, item_back = lax.optimization_barrier(
        (arrived, near, far, counts, linked, codes, far_codes, hand, target, item_back)
    )
    if items:
        passed, target, item_back = relay(hand, arrived, target, item_back, direct, items)
        gained = exchange(passed, chips)
    back, best = score(codes, counts, linked, near, far, arrived, 16, False)
    places = direct
    if items:
        gained = gained.reshape(CLASSES, chips // CLASSES * relayed, depth)
        far_back, far_best = score(far_codes, counts, linked, near, far, gained, 4, True)
        best = jnp.maximum(best, far_best)
        hit = item_back.reshape(turns(direct), CLASSES, chips)[..., None] == jnp.arange(relayed, dtype=jnp.int32)
        far_back = far_back.reshape(1, CLASSES, 1, relayed, UNIT)
        far_back = jnp.where(hit[..., None], far_back, -1.0).max(axis=3)
        far_back = far_back.transpose(2, 0, 1, 3).reshape(chips, -1)
        back = jnp.concatenate([back, far_back], axis=1)
        places = direct + turns(direct) * CLASSES
    returned = exchange(back, chips)
    spots = target.T.reshape(-1)
    values = returned.reshape(-1, UNIT).T
    hit = spots[:, None] == jnp.arange(2 * blocks * width // UNIT, dtype=jnp.int32)[None, :]
    folded = jnp.where(hit[None], values[:, :, None], -1.0).max(axis=1)
    best = jnp.maximum(best, folded.T.reshape(2 * blocks, width))
    other = lax.ppermute(best[blocks:], "shard", [(d, d ^ 1) for d in range(2 * chips)])
    return jnp.maximum(best[:blocks], other)


def on_device(embeddings, block_rows, pairs):
    blocks = block_rows.shape[0]
    width = embeddings.shape[0] // blocks
    peers = lax.axis_size("shard")
    myself = lax.axis_index("shard")
    swap = [(d, d ^ 1) for d in range(peers)]
    row_block, col_block = pairs[:, 0], pairs[:, 1]
    alive = pairs[:, 2] == myself
    owner = row_block // blocks
    remote = alive & (owner != myself)
    row_local, col_local = row_block % blocks, col_block % blocks
    tell = ask(myself, pairs, block_rows, peers)
    told = lax.all_to_all(tell, "shard", split_axis=0, concat_axis=0, tiled=True)[:, 0]

    unit = normalize(embeddings, tell)
    near = unit.reshape(blocks, width, -1)
    far = lax.ppermute(near, "shard", swap)

    nearby = alive & ~remote
    row_table = one_hot(row_local, blocks, nearby).astype(jnp.float32)
    col_table = one_hot(col_local, blocks, nearby).astype(jnp.float32)
    adjacency = (
        lax.dot_general(row_table, col_table, (((0,), (0,)), ((), ())), preferred_element_type=jnp.float32) > 0.5
    )
    linked = (adjacency | adjacency.T).astype(jnp.int32).reshape(-1)

    plan = make_plan(*PLANS[0], told, myself)
    counts = jnp.concatenate([block_rows, lax.dynamic_slice_in_dim(told, myself ^ 1, 1, 0)[0, peers:]])

    def attempt(level, plan):
        def here():
            return far_maxima(*PLANS[level], plan, counts, linked, near, far)

        def later():
            return attempt(level + 1, make_plan(*PLANS[level + 1], told, myself))

        return lax.cond(plan[-1][0] > 0, here, later) if level + 1 < len(PLANS) else here()

    return attempt(0, plan)


def solution(mesh):
    placed = (P("shard", None), P("shard"), P("shard", None))
    return jax.shard_map(
        on_device, mesh=mesh, in_specs=placed, out_specs=P("shard", None), check_vma=False
    )
```

```python
import functools

import jax
import jax.numpy as jnp
import numpy as np
from jax import lax
from jax.experimental import pallas as pl
from jax.experimental.pallas import tpu as pltpu
from jax.sharding import PartitionSpec as P

UNIT = 16
CLASSES = 4
COLORS = 2 * CLASSES
LOG_COLORS = 3
PLANS = ((7, 16, 24), (8, 16, 16), (16, 0, 0))
SHARE = 8
MIB = 1024 * 1024


def turns(direct):
    return -(-(2 * 16 - 2 * direct) // COLORS)


def ask_kernel(me_ref, pairs_ref, rows_ref, tell_ref):
    device = me_ref[0]
    peers, _, columns = tell_ref.shape
    row, col = pairs_ref[0:1, :], pairs_ref[1:2, :]
    owner = row >> 4
    far = (pairs_ref[2:3, :] == device) & (owner != device)
    peer = lax.broadcasted_iota(jnp.int32, (peers, row.shape[1]), 0)
    code = (row & 15) * 16 + (col & 15)
    code = jnp.where((owner == peer) & far, code, -1).astype(jnp.float32)
    most = code[:, :peers]
    for k in range(1, row.shape[1] // peers):
        most = jnp.maximum(most, code[:, k * peers : (k + 1) * peers])
    wanted = jnp.max(most.T, axis=0, keepdims=True).astype(jnp.int32)
    tell = jnp.concatenate([wanted, rows_ref[...]], axis=1)
    tell_ref[...] = jnp.broadcast_to(tell[None], tell_ref.shape)


def ask(device, pairs, block_rows, peers):
    blocks = block_rows.shape[0]
    assert blocks == 16
    vmem = pl.BlockSpec(memory_space=pltpu.VMEM)
    return pl.pallas_call(
        ask_kernel,
        in_specs=[pl.BlockSpec(memory_space=pltpu.SMEM), vmem, vmem],
        out_specs=vmem,
        out_shape=jax.ShapeDtypeStruct((peers, 1, peers + blocks), jnp.int32),
        name="ask",
    )(device.reshape(1), pairs.T, block_rows.reshape(1, blocks))


def normalize_kernel(after_ref, values_ref, unit_ref):
    values = values_ref[...].astype(jnp.float32)
    total = jnp.sum(values * values, axis=-1, keepdims=True)
    unit_ref[...] = (values * lax.rsqrt(total + 1e-06)).astype(jnp.bfloat16)


def normalize(embeddings, after):
    rows, depth = embeddings.shape
    step = 1024
    return pl.pallas_call(
        normalize_kernel,
        grid=(rows // step,),
        in_specs=[pl.BlockSpec(memory_space=pl.ANY), pl.BlockSpec((step, depth), lambda i: (i, 0))],
        out_specs=pl.BlockSpec((step, depth), lambda i: (i, 0)),
        out_shape=jax.ShapeDtypeStruct((rows, depth), jnp.bfloat16),
        cost_estimate=pl.CostEstimate(flops=4 * rows * depth, bytes_accessed=4 * rows * depth, transcendentals=rows),
        name="normalize",
    )(after, embeddings)


def near_pairs(blocks):
    return np.array([(i, j) for i in range(blocks // 4) for j in range(blocks // 2) if (j + 1) * 2 > i * 4], np.int32)


def score_near(near, linked, counts, rows_ref, best_ref, kept):
    blocks, width, depth = rows_ref.shape[0] // 2, rows_ref.shape[1], rows_ref.shape[2]
    kept[...] = jnp.full(kept.shape, -1.0, jnp.float32)
    i = lax.broadcasted_iota(jnp.int32, (width, width), 0)
    j = lax.broadcasted_iota(jnp.int32, (width, width), 1)

    def step(number, carry):
        left, right = near[2 * number], near[2 * number + 1]
        rows = rows_ref[pl.ds(left * 4, 4)].reshape(4 * width, depth)
        cols = rows_ref[pl.ds(right * 2, 2)].reshape(2 * width, depth)
        scores = lax.dot_general(rows, cols, (((1,), (1,)), ((), ())), preferred_element_type=jnp.float32)
        for b in range(2):
            c = right * 2 + b
            most = best_ref[pl.ds(c, 1), :]
            for a in range(4):
                r = left * 4 + a
                limit = jnp.where(linked[r * blocks + c] > 0, counts[r], 0)
                keep = (i < limit) & (j < counts[c]) & ((r != c) | (i != j))
                part = jnp.where(keep, scores[a * width : (a + 1) * width, b * width : (b + 1) * width], -1.0)
                kept[r] = jnp.maximum(kept[r], part)
                most = jnp.maximum(most, jnp.max(part, axis=0, keepdims=True))
            best_ref[pl.ds(c, 1), :] = most
        return carry

    lax.fori_loop(0, len(near_pairs(blocks)), step, 0)
    for b in range(blocks):
        best_ref[pl.ds(b, 1), :] = jnp.maximum(best_ref[pl.ds(b, 1), :], jnp.max(kept[b].T, axis=0, keepdims=True))


def exact_dot(a, b):
    return jnp.dot(
        a.astype(jnp.float32).astype(jnp.bfloat16),
        b.astype(jnp.float32).astype(jnp.bfloat16),
        preferred_element_type=jnp.float32,
    ).astype(jnp.int32)


def flip(a):
    return a.astype(jnp.float32).T.astype(jnp.int32)


def plan_kernel(
    direct, items, relayed, chips, me_ref, pair_ref, count_ref, count_t_ref,
    send_ref, far_ref, code_ref, far_code_ref, hand_ref, target_ref, back_ref, fits_ref,
    w_lo, w_hi, sums, mine,
):
    device = me_ref[0]
    chip, core = device // 2, device % 2
    devices = 2 * chips
    flat = (chips, chips)
    pair = pair_ref[...]
    code = jnp.maximum(pair, 0)
    row_of, col_of = code >> 4, code & 15
    row_count = jnp.zeros(pair.shape, jnp.int32)
    col_count = jnp.zeros(pair.shape, jnp.int32)
    for l in range(16):
        row_count = jnp.where(row_of == l, count_t_ref[pl.ds(l, 1), :], row_count)
        col_count = jnp.where(col_of == l, count_ref[:, l : l + 1], col_count)

    xs = lax.broadcasted_iota(jnp.int32, (chips, devices), 0)
    ds = lax.broadcasted_iota(jnp.int32, (chips, devices), 1)
    pick = [(ds == 2 * xs + i).astype(jnp.int32) for i in range(2)]
    pick_t = [flip(p) for p in pick]

    def split(values):
        half = [exact_dot(p, values) for p in pick]
        return [[exact_dot(half[i], pick_t[j]) for j in range(2)] for i in range(2)]

    asked = {"code": split(pair + 1), "row": split(row_count), "col": split(col_count)}
    asked_t = {k: [[flip(v[j][i]) for j in range(2)] for i in range(2)] for k, v in asked.items()}

    x = lax.broadcasted_iota(jnp.int32, flat, 0)
    y = lax.broadcasted_iota(jnp.int32, flat, 1)
    low, same = x <= y, x == y
    edges = []
    for kind in range(2):
        for p in range(2):
            for q in range(2):
                first, second = (asked_t, asked) if kind == 0 else (asked, asked_t)
                here = {k: jnp.where(low, first[k][p][q], second[k][q][p]) for k in asked}
                exists = here["code"] > 0
                if kind == 1:
                    exists = exists & ~same
                number = jnp.maximum(here["code"] - 1, 0)
                r, c = number >> 4, number & 15
                side = jnp.where(low, p, q) * 16
                other = jnp.where(low, q, p) * 16
                owns_row = low if kind == 0 else ~low
                own_block = side + jnp.where(owns_row, r, c)
                other_block = other + jnp.where(owns_row, c, r)
                own_rows = jnp.where(exists, jnp.where(owns_row, here["row"], here["col"]), 0)
                other_rows = jnp.where(exists, jnp.where(owns_row, here["col"], here["row"]), 0)
                edges.append((exists, own_block, other_block, own_rows, other_rows))
    for e, (exists, _, _, own_rows, other_rows) in enumerate(edges):
        own_units, other_units = (own_rows + 15) >> 4, (other_rows + 15) >> 4
        w_lo[e] = jnp.where(low, own_units, other_units)
        w_hi[e] = jnp.where(low, other_units, own_units)

    for half in range(2):
        for choice in range(16):
            up = jnp.zeros(flat, jnp.int32)
            down = jnp.zeros(flat, jnp.int32)
            for b in range(4):
                if choice >> b & 1:
                    up = up + w_lo[half * 4 + b]
                else:
                    down = down + w_hi[half * 4 + b]
            lanes = pl.ds(0, chips) if half or choice < 8 else pl.ds(chips, chips)
            spot = choice if half else choice % 8
            sums[half, spot, :, lanes] = up
            sums[2 + half, spot, :, lanes] = down
            if half:
                sums[1, spot, :, pl.ds(chips, chips)] = up
                sums[3, spot, :, pl.ds(chips, chips)] = down
    eight = jnp.where(lax.broadcasted_iota(jnp.int32, (chips, devices), 1) < chips, 0, 8)

    def try_half(a, least):
        up_a, down_a = sums[0, a] - 2 * direct, sums[2, a] - 2 * direct
        for b in range(16):
            up, down = up_a + sums[1, b], down_a + sums[3, b]
            over = jnp.maximum(up, 0) + jnp.maximum(down, 0)
            rank = over * 65536 + jnp.maximum(up, down) * 256 + (b * 16 + a) + eight
            least = jnp.minimum(least, rank)
        return least

    least = lax.fori_loop(0, 8, try_half, jnp.full((chips, devices), 2**30, jnp.int32))
    least = jnp.minimum(least[:, :chips], least[:, chips:])
    chosen = jnp.where(same, 255, least & 255)

    out_total = jnp.zeros(flat, jnp.int32)
    in_total = jnp.zeros(flat, jnp.int32)
    for e, (exists, own_block, other_block, own_rows, other_rows) in enumerate(edges):
        bit = (chosen >> e) & 1
        sends = exists & ((bit == 1) == low)
        out_units = jnp.where(sends, (own_rows + 15) >> 4, 0)
        in_rows = jnp.where(same, own_rows, other_rows)
        in_units = jnp.where((exists & ~sends) | same, (in_rows + 15) >> 4, 0)
        out_total = out_total + out_units
        in_total = in_total + in_units
        mine[e] = out_units
        mine[8 + e] = own_block ^ (core * 16)
        mine[16 + e] = in_units
        mine[24 + e] = jnp.where(same, other_block, own_block) ^ (core * 16)
        mine[32 + e] = in_rows
    mine[40] = out_total
    mine[41] = in_total

    far = jnp.maximum(out_total - 2 * direct, 0)
    before = exact_dot(far, (x < y).astype(jnp.int32))
    total = jnp.sum(far, axis=1, keepdims=True)
    at_self = jnp.sum(jnp.where(same, before, 0), axis=1, keepdims=True)
    rank = before - at_self + jnp.where(y < x, total, 0)
    over_out = jnp.max((total + COLORS - 1) >> LOG_COLORS)
    over_in = jnp.zeros((), jnp.int32)
    earlier = (y < x).astype(jnp.int32)
    number, place, first = [], [], []
    for color in range(COLORS):
        first.append((color - rank) & (COLORS - 1))
        number.append((far - first[-1] + COLORS - 1) >> LOG_COLORS)
        over_in = jnp.maximum(over_in, jnp.max(jnp.sum(number[-1], axis=0, keepdims=True)))
        place.append(exact_dot(earlier, number[-1]))
    room = turns(direct)
    fits = (over_out <= items) & (over_in <= relayed) & (jnp.max(far) <= room * COLORS)
    fits_ref[0] = fits.astype(jnp.int32)
    odd = core == 1
    own_class = chip // (chips // CLASSES)
    hand_number = jnp.zeros(flat, jnp.int32)
    hand_place = jnp.zeros(flat, jnp.int32)
    hand_first = jnp.zeros(flat, jnp.int32)
    for k in range(CLASSES):
        picked = [jnp.where(odd, v[2 * k + 1], v[2 * k]) for v in (number, place, first)]
        for n, v in enumerate(picked):
            mine[47 + 6 * k + n] = flip(v)
        here = own_class == k
        hand_number = jnp.where(here, picked[0], hand_number)
        hand_place = jnp.where(here, picked[1], hand_place)
        hand_first = jnp.where(here, picked[2], hand_first)
    mine[42] = rank
    mine[43] = far
    own = pl.ds(chip, 1)

    out_units = [mine[e, own, :] for e in range(SHARE)]
    out_block = [mine[8 + e, own, :] for e in range(SHARE)]
    in_units = [mine[16 + e, own, :] for e in range(SHARE)]
    in_block = [mine[24 + e, own, :] for e in range(SHARE)]
    in_rows = [mine[32 + e, own, :] for e in range(SHARE)]
    out_total, in_total, rank_own, far_own = (mine[40 + k, own, :] for k in range(4))

    def lane(total):
        plain = jnp.minimum(total, 2 * direct)
        half = (plain + 1) >> 1
        return jnp.where(odd, half, 0), jnp.where(odd, plain - half, half)

    def unit_at(position, valid):
        value = jnp.full(position.shape, -1, jnp.int32)
        start = jnp.zeros((1, chips), jnp.int32)
        for e in range(SHARE):
            hit = valid & (position >= start) & (position < start + out_units[e])
            value = jnp.where(hit, out_block[e] * 8 + position - start, value)
            start = start + out_units[e]
        return value

    def code_at(position, valid):
        value = jnp.zeros(position.shape, jnp.int32)
        start = jnp.zeros((1, chips), jnp.int32)
        for e in range(SHARE):
            hit = valid & (position >= start) & (position < start + in_units[e])
            rows = jnp.minimum(in_rows[e] - UNIT * (position - start), UNIT)
            value = jnp.where(hit, in_block[e] * 32 + 32 + rows, value)
            start = start + in_units[e]
        return value

    step = lax.broadcasted_iota(jnp.int32, (direct, chips), 0)
    begin, length = lane(out_total)
    plain = unit_at(begin + step, step < length)
    send_ref[...] = jnp.maximum(plain, 0)
    target_ref[pl.ds(0, direct), :] = plain
    begin, length = lane(in_total)
    code_ref[...] = code_at(begin + step, step < length)

    if items:
        slot = lax.broadcasted_iota(jnp.int32, (items, chips), 0)
        place_in = lax.broadcasted_iota(jnp.int32, (relayed, chips), 0)
        for k in range(CLASSES):
            turn = COLORS * slot + 2 * k + core - rank_own
            unit = unit_at(2 * direct + turn, (turn >= 0) & (turn < far_own))
            far_ref[:, k : k + 1] = jnp.sum(jnp.maximum(unit, 0), axis=1, keepdims=True)
            number_t, place_t, first_t = (mine[47 + 6 * k + n, own, :] for n in range(3))
            made = jnp.zeros((relayed, chips), jnp.int32)
            for n in range(room):
                first = (2 * k + core - rank_own) & (COLORS - 1)
                target_ref[pl.ds(direct + CLASSES * n + k, 1), :] = unit_at(
                    2 * direct + first + COLORS * n, n < (far_own - first + COLORS - 1) >> LOG_COLORS
                )
                back_ref[pl.ds(CLASSES * n + k, 1), :] = jnp.where(n < number_t, place_t + n, -1)
                hit = (place_t + n == place_in) & (n < number_t)
                made = made + code_at(2 * direct + first_t + COLORS * n + 0 * place_in, hit)
            far_code_ref[:, k : k + 1] = jnp.sum(made, axis=1, keepdims=True)
        hand_number, hand_place, hand_from = (
            flip(hand_number), flip(hand_place), flip((rank + hand_first) >> LOG_COLORS)
        )
        for q in range(relayed):
            value = jnp.zeros(flat, jnp.int32)
            for n in range(room):
                hit = (hand_place + n == q) & (n < hand_number)
                value = value + jnp.where(hit, y * items + hand_from + n, 0)
            hand_ref[:, q : q + 1] = jnp.sum(value, axis=1, keepdims=True)


def make_plan(direct, items, relayed, told, device):
    devices, columns = told.shape
    chips = devices // 2
    ints = lambda *shape: jax.ShapeDtypeStruct(shape, jnp.int32)
    vmem = pl.BlockSpec(memory_space=pltpu.VMEM)
    return pl.pallas_call(
        functools.partial(plan_kernel, direct, items, relayed, chips),
        in_specs=[pl.BlockSpec(memory_space=pltpu.SMEM), vmem, vmem, vmem],
        out_specs=[vmem] * 7 + [pl.BlockSpec(memory_space=pltpu.SMEM)],
        out_shape=[
            ints(direct, chips),
            ints(max(items, 8), CLASSES),
            ints(direct, chips),
            ints(max(relayed, 8), CLASSES),
            ints(chips, max(relayed, 8)),
            ints(direct + turns(direct) * CLASSES, chips),
            ints(max(turns(direct), 1) * CLASSES, chips),
            ints(1),
        ],
        scratch_shapes=[
            pltpu.VMEM((SHARE, chips, chips), jnp.int32),
            pltpu.VMEM((SHARE, chips, chips), jnp.int32),
            pltpu.VMEM((4, 16, chips, devices), jnp.int32),
            pltpu.VMEM((44 + 6 * CLASSES, chips, chips), jnp.int32),
        ],
        compiler_params=pltpu.CompilerParams(vmem_limit_bytes=32 * MIB),
        cost_estimate=pl.CostEstimate(flops=10**11, bytes_accessed=10**6, transcendentals=0),
        name="plan",
    )(device.reshape(1), told[:, :devices], told[:, devices:], told[:, devices:].T)


def turning(first, second):
    rows = first * second
    o = lax.broadcasted_iota(jnp.int32, (rows, rows), 0)
    i = lax.broadcasted_iota(jnp.int32, (rows, rows), 1)
    return ((o % first) * second + o // first == i).astype(jnp.float32).astype(jnp.bfloat16)


def turn(take, values):
    return jnp.dot(take, values, preferred_element_type=jnp.float32).astype(jnp.bfloat16)


def fetch(near_ref, far_ref, held, sems):
    half = near_ref.shape[0]
    copies = [
        pltpu.make_async_copy(near_ref, held.at[pl.ds(0, half)], sems.at[0]),
        pltpu.make_async_copy(far_ref, held.at[pl.ds(half, half)], sems.at[1]),
    ]
    for copy in copies:
        copy.start()
    for copy in copies:
        copy.wait()


def pack_kernel(group, direct, items, send, far, near_ref, far_ref, out_ref, held, gathered, turned, sems):
    step = pl.program_id(0)
    chips = pl.num_programs(0) * group

    @pl.when(step == 0)
    def _():
        fetch(near_ref, far_ref, held, sems)
        if items:
            take = turning(items, UNIT)
            for p in range(CLASSES):
                for q in range(items):
                    gathered[pl.ds(q * UNIT, UNIT), :] = held[far[q * CLASSES + p]]
                size = items * UNIT
                turned[pl.ds(p * size, size), :] = turn(take, gathered[...])

    for k in range(group):
        slot = step * group + k
        for p in range(direct):
            out_ref[k, pl.ds(p * UNIT, UNIT), :] = held[send[p * chips + slot]]
        if items:
            out_ref[k, pl.ds(direct * UNIT, items), :] = turned[pl.ds(pl.multiple_of(slot * items, items), items), :]


def pack(direct, items, send, far, near_units, far_units):
    units, _, depth = near_units.shape
    chips = send.shape[1]
    rows = direct * UNIT + items
    group = 8 if items else 4
    some = max(items, 16)
    return pl.pallas_call(
        functools.partial(pack_kernel, group, direct, items),
        grid_spec=pltpu.PrefetchScalarGridSpec(
            num_scalar_prefetch=2,
            grid=(chips // group,),
            in_specs=[pl.BlockSpec(memory_space=pl.ANY)] * 2,
            out_specs=pl.BlockSpec((group, rows, depth), lambda i, *_: (i, 0, 0)),
            scratch_shapes=[
                pltpu.VMEM((2 * units, UNIT, depth), jnp.bfloat16),
                pltpu.VMEM((some * UNIT, depth), jnp.bfloat16),
                pltpu.VMEM((some * chips, depth), jnp.bfloat16),
                pltpu.SemaphoreType.DMA((2,)),
            ],
        ),
        out_shape=jax.ShapeDtypeStruct((chips, rows, depth), jnp.bfloat16),
        compiler_params=pltpu.CompilerParams(vmem_limit_bytes=20 * MIB),
        name="pack",
    )(send.reshape(-1), far.reshape(-1), near_units, far_units)


def relay_kernel(hand_ref, held_ref, target_ref, back_ref, out_ref, target_out, back_out):
    target_out[...] = target_ref[...]
    back_out[...] = back_ref[...]
    held = held_ref[...]
    rows = held.shape[0] * held.shape[1]
    hand = hand_ref[...]
    slots, relayed = hand.shape
    o = lax.broadcasted_iota(jnp.int32, (slots * relayed, slots), 0)
    spread = (o // relayed == lax.broadcasted_iota(jnp.int32, o.shape, 1)).astype(jnp.int32)
    each = exact_dot(spread, hand >> 4) * 16 + exact_dot(spread, hand & 15)
    o = lax.broadcasted_iota(jnp.int32, each.shape, 0)
    own = o % relayed == lax.broadcasted_iota(jnp.int32, each.shape, 1)
    source = jnp.sum(jnp.where(own, each, 0), axis=1, keepdims=True)
    i = lax.broadcasted_iota(jnp.int32, (out_ref.shape[0], rows), 1)
    take = (source == i).astype(jnp.float32).astype(jnp.bfloat16)
    out_ref[...] = jnp.dot(
        take, held.reshape(rows, held.shape[2]), preferred_element_type=jnp.float32
    ).astype(jnp.bfloat16)


def relay(hand, arrived, target, back, direct, items):
    chips, relayed = hand.shape
    depth = arrived.shape[2]
    step = chips * relayed // 2
    tables = [pl.BlockSpec(t.shape, lambda i: (0, 0)) for t in (target, back)]
    passed, target, back = pl.pallas_call(
        relay_kernel,
        grid=(chips * relayed // step,),
        in_specs=[
            pl.BlockSpec((chips // 2, relayed), lambda i: (i, 0)),
            pl.BlockSpec((chips, items, depth), lambda i: (0, direct * UNIT // items, 0)),
            *tables,
        ],
        out_specs=[pl.BlockSpec((step, depth), lambda i: (i, 0)), *tables],
        out_shape=[
            jax.ShapeDtypeStruct((chips * relayed, depth), jnp.bfloat16),
            jax.ShapeDtypeStruct(target.shape, jnp.int32),
            jax.ShapeDtypeStruct(back.shape, jnp.int32),
        ],
        compiler_params=pltpu.CompilerParams(vmem_limit_bytes=54 * MIB),
        name="relay",
    )(hand, arrived, target, back)
    return passed.reshape(chips, relayed, depth), target, back


def score_kernel(
    places, group, turned, codes, counts, near, linked, near_ref, far_ref, arrived_ref, back_ref, best_ref,
    held, rows_held, batch, tiles, kept, head, follow, sems,
):
    slots = back_ref.shape[0]
    blocks, width, _ = held.shape
    copies = [
        pltpu.make_async_copy(near_ref, held.at[pl.ds(0, blocks // 2)], sems.at[0]),
        pltpu.make_async_copy(far_ref, held.at[pl.ds(blocks // 2, blocks // 2)], sems.at[1]),
    ]
    if turned:
        copies.insert(0, pltpu.make_async_copy(arrived_ref, rows_held, sems.at[2]))
    else:
        copies.append(pltpu.make_async_copy(arrived_ref.at[:, pl.ds(0, places * UNIT)], rows_held, sems.at[2]))
    for copy in copies:
        copy.start()
    best_ref[...] = jnp.full(best_ref.shape, -1.0, jnp.float32)
    tiles[...] = jnp.full(tiles.shape, -1.0, jnp.float32)

    def clear(b, carry):
        head[b] = -1
        return carry

    lax.fori_loop(0, blocks, clear, 0)

    def link(slot, carry):
        for p in range(places):
            made = codes[p * slots + slot]
            block = jnp.maximum((made >> 5) - 1, 0)
            unit = slot * 32 + p

            @pl.when(made > 0)
            def _():
                follow[unit] = head[block]
                head[block] = unit

        return carry

    lax.fori_loop(0, slots, link, 0)
    if turned:
        take = turning(UNIT, places)
    copies[0].wait()
    if turned:
        for slot in range(slots):
            rows_held[slot] = turn(take, rows_held[slot])
    else:
        score_near(near, linked, counts, held, best_ref, kept)
    for copy in copies[1:]:
        copy.wait()

    i = lax.broadcasted_iota(jnp.int32, (UNIT, width), 0)
    j = lax.broadcasted_iota(jnp.int32, (UNIT, width), 1)

    def per_block(block, carry):
        columns = j < counts[block]

        def some_units(unit):
            taken = []
            for g in range(group):
                live = unit >= 0
                here = jnp.maximum(unit, 0)
                slot, p = here >> 5, here & 31
                batch[pl.ds(g * UNIT, UNIT), :] = rows_held[slot, pl.ds(pl.multiple_of(p * UNIT, UNIT), UNIT), :]
                rows = jnp.where(live, codes[p * slots + slot] & 31, 0)
                taken.append((jnp.where(live, slot, slots), p, rows))
                unit = jnp.where(live, follow[here], -1)
            scores = lax.dot_general(
                batch[...], held[block], (((1,), (1,)), ((), ())), preferred_element_type=jnp.float32
            )
            most = best_ref[pl.ds(block, 1), :]
            for g, (slot, p, rows) in enumerate(taken):
                tile = jnp.where((i < rows) & columns, scores[g * UNIT : (g + 1) * UNIT], -1.0)
                tiles[slot, pl.ds(pl.multiple_of(p * UNIT, UNIT), UNIT), :] = tile
                most = jnp.maximum(most, jnp.max(tile, axis=0, keepdims=True))
            best_ref[pl.ds(block, 1), :] = most
            return unit

        lax.while_loop(lambda unit: unit >= 0, some_units, head[block])
        return carry

    lax.fori_loop(0, blocks, per_block, 0)

    if slots % 8 == 0:

        def finish(part, carry):
            for k in range(8):
                slot = part * 8 + k
                back_ref[pl.ds(slot, 1), :] = jnp.max(tiles[slot].T, axis=0, keepdims=True)
            return carry

        lax.fori_loop(0, slots // 8, finish, 0)
    else:
        for slot in range(slots):
            back_ref[slot : slot + 1, :] = jnp.max(tiles[slot].T, axis=0, keepdims=True)


def score(codes, counts, linked, near, far, arrived, group, turned):
    blocks, width, depth = near.shape
    places, slots = codes.shape
    rows = places * UNIT
    any_place = pl.BlockSpec(memory_space=pl.ANY)
    vmem = pl.BlockSpec(memory_space=pltpu.VMEM)
    smem = pl.BlockSpec(memory_space=pltpu.SMEM)
    return pl.pallas_call(
        functools.partial(score_kernel, places, group, turned),
        in_specs=[smem, smem, smem, smem, any_place, any_place, any_place],
        out_specs=[vmem, vmem],
        out_shape=[
            jax.ShapeDtypeStruct((slots, rows), jnp.float32),
            jax.ShapeDtypeStruct((2 * blocks, width), jnp.float32),
        ],
        scratch_shapes=[
            pltpu.VMEM((2 * blocks, width, depth), jnp.bfloat16),
            pltpu.VMEM((slots, rows, depth), jnp.bfloat16),
            pltpu.VMEM((group * UNIT, depth), jnp.bfloat16),
            pltpu.VMEM((slots + 1, rows, width), jnp.float32),
            pltpu.VMEM((8 if turned else blocks, width, width), jnp.float32),
            pltpu.SMEM((2 * blocks,), jnp.int32),
            pltpu.SMEM((slots * 32,), jnp.int32),
            pltpu.SemaphoreType.DMA((3,)),
        ],
        compiler_params=pltpu.CompilerParams(vmem_limit_bytes=(24 if turned else 45 if places <= 8 else 56) * MIB),
        cost_estimate=pl.CostEstimate(
            flops=2 * slots * rows * width * depth, bytes_accessed=2 * slots * rows * depth, transcendentals=0
        ),
        name="score",
    )(codes.reshape(-1), counts, jnp.asarray(near_pairs(blocks).reshape(-1)), linked, near, far, arrived)


def one_hot(index, count, valid):
    return (index[:, None] == jnp.arange(count, dtype=jnp.int32)[None, :]) & valid[:, None]


def exchange(values, chips):
    groups = [[2 * x + c for x in range(chips)] for c in range(2)]
    return lax.all_to_all(values, "shard", split_axis=0, concat_axis=0, axis_index_groups=groups, tiled=True)


def far_maxima(direct, items, relayed, plan, counts, linked, near, far):
    send, own_far, codes, far_codes, hand, target, item_back, _ = plan
    blocks, width, depth = near.shape
    chips = send.shape[1]
    outgoing = pack(
        direct, items, send, own_far,
        near.reshape(-1, UNIT, depth), far.reshape(-1, UNIT, depth),
    )
    arrived = exchange(outgoing, chips)
    arrived, near, far, counts, linked, codes, far_codes, hand, target, item_back = lax.optimization_barrier(
        (arrived, near, far, counts, linked, codes, far_codes, hand, target, item_back)
    )
    if items:
        passed, target, item_back = relay(hand, arrived, target, item_back, direct, items)
        gained = exchange(passed, chips)
    back, best = score(codes, counts, linked, near, far, arrived, 16, False)
    places = direct
    if items:
        gained = gained.reshape(CLASSES, chips // CLASSES * relayed, depth)
        far_back, far_best = score(far_codes, counts, linked, near, far, gained, 4, True)
        best = jnp.maximum(best, far_best)
        hit = item_back.reshape(turns(direct), CLASSES, chips)[..., None] == jnp.arange(relayed, dtype=jnp.int32)
        far_back = far_back.reshape(1, CLASSES, 1, relayed, UNIT)
        far_back = jnp.where(hit[..., None], far_back, -1.0).max(axis=3)
        far_back = far_back.transpose(2, 0, 1, 3).reshape(chips, -1)
        back = jnp.concatenate([back, far_back], axis=1)
        places = direct + turns(direct) * CLASSES
    returned = exchange(back, chips)
    spots = target.T.reshape(-1)
    values = returned.reshape(-1, UNIT).T
    hit = spots[:, None] == jnp.arange(2 * blocks * width // UNIT, dtype=jnp.int32)[None, :]
    folded = jnp.where(hit[None], values[:, :, None], -1.0).max(axis=1)
    best = jnp.maximum(best, folded.T.reshape(2 * blocks, width))
    other = lax.ppermute(best[blocks:], "shard", [(d, d ^ 1) for d in range(2 * chips)])
    return jnp.maximum(best[:blocks], other)


def on_device(embeddings, block_rows, pairs):
    blocks = block_rows.shape[0]
    width = embeddings.shape[0] // blocks
    peers = lax.axis_size("shard")
    myself = lax.axis_index("shard")
    swap = [(d, d ^ 1) for d in range(peers)]
    row_block, col_block = pairs[:, 0], pairs[:, 1]
    alive = pairs[:, 2] == myself
    owner = row_block // blocks
    remote = alive & (owner != myself)
    row_local, col_local = row_block % blocks, col_block % blocks
    tell = ask(myself, pairs, block_rows, peers)
    told = lax.all_to_all(tell, "shard", split_axis=0, concat_axis=0, tiled=True)[:, 0]

    unit = normalize(embeddings, tell)
    near = unit.reshape(blocks, width, -1)
    far = lax.ppermute(near, "shard", swap)

    nearby = alive & ~remote
    row_table = one_hot(row_local, blocks, nearby).astype(jnp.float32)
    col_table = one_hot(col_local, blocks, nearby).astype(jnp.float32)
    adjacency = (
        lax.dot_general(row_table, col_table, (((0,), (0,)), ((), ())), preferred_element_type=jnp.float32) > 0.5
    )
    linked = (adjacency | adjacency.T).astype(jnp.int32).reshape(-1)

    plan = make_plan(*PLANS[0], told, myself)
    counts = jnp.concatenate([block_rows, lax.dynamic_slice_in_dim(told, myself ^ 1, 1, 0)[0, peers:]])

    def attempt(level, plan):
        def here():
            return far_maxima(*PLANS[level], plan, counts, linked, near, far)

        def later():
            return attempt(level + 1, make_plan(*PLANS[level + 1], told, myself))

        return lax.cond(plan[-1][0] > 0, here, later) if level + 1 < len(PLANS) else here()

    return attempt(0, plan)


def solution(mesh):
    placed = (P("shard", None), P("shard"), P("shard", None))
    return jax.shard_map(
        on_device, mesh=mesh, in_specs=placed, out_specs=P("shard", None), check_vma=False
    )
```
